32 devices in a mesh: box: 8 (over z, y), dir: 4 (over x, core).
Axes of the slice: x: 2, y: 2, z: 4, core: 2. Of those that a mesh axis runs over, the one named last changes fastest.
Arguments:
- pattern: bfloat16 [2, 32, 16, 128, 256], P(None, 'box', None, 'dir'), may hold values from -6 to 6
- occupied: int32 [32, 16], P('box'), may hold values from 0 to 1, as said below
- trans_fine: bfloat16 [2, 40, 128, 256], P(None, None, 'dir'), may hold values from -1.25 to 1.25
- trans_coarse: bfloat16 [2, 40, 256, 512], P(None, None, 'dir'), may hold values from -1.25 to 1.25
- theta_weights: bfloat16 [256, 4], P('dir'), may hold values from -0.19921875 to 0.796875
- phi_matrix: bfloat16 [256, 512], replicated, may hold values from -0.375 to 0.375
- child_phase: float32 [4, 256, 512], P(None, 'dir'), may hold values from -3.140625 to 3.140625
Outputs:
- local_fine: bfloat16 [2, 32, 16, 128, 256], P(None, 'box', None, 'dir')
- local_coarse: bfloat16 [2, 16, 8, 256, 512], P(None, 'box', None, 'dir')
The draws below stay inside these ranges and needn't reach their ends.
Inputs may be any that keep to these rules, and one draw needn't show every extreme that they name: `occupied`: 1 for a box that holds unknowns, 0 for an empty one.
All inputs are finite; a program needn't handle non-finite values.
Results may differ from the reference program's by a relative error of at most 0.0057.
Values may be sent and summed in bfloat16 or wider, within the bound.
No kernel may reach another device: no remote copies, remote signals or barrier semaphores. Data moves between devices by JAX's collectives and lax.ppermute only.
A program may use at most 320 MiB of HBM per device.

```python
import jax
import jax.numpy as jnp
from jax import lax

RX = 4
NBY = 16
NTH1 = 128
NPH1 = 256
FAR = 40
NTH2 = 256
NPH2 = 512
NBX = 32


def draw_occupied(key, part):
    first_key = jax.random.fold_in(key, 11)
    second_key = jax.random.fold_in(key, 23)
    levels = jax.random.randint(first_key, (NBX // RX, 1, 1), 1, 5)
    levels = jnp.broadcast_to(levels, (NBX // RX, RX, NBY)).reshape(NBX, NBY)
    draws = jax.random.randint(second_key, (NBX, NBY), 0, 4)
    return (draws < levels).astype(jnp.int32)


def block_levels(stream_key, shape, shards, least, top_value):
    factor_of, own = 1.0, jax.random.fold_in(stream_key, 6)
    for dim, blocks in shards:
        steps = jnp.exp(jax.random.uniform(jax.random.fold_in(own, dim), (blocks,), jnp.float32, least / len(shards), top_value / len(shards)))
        factor_of = factor_of * jnp.repeat(steps, shape[dim] // blocks).reshape([-1 if axis == dim else 1 for axis in range(len(shape))])
    return factor_of


def normal_values(own_key, extent, deviation, limit, split=(), kind=jnp.bfloat16):
    level = block_levels(own_key, extent, split, -0.22, 0.18) if split else 1.0
    entries = jax.random.normal(own_key, extent, jnp.float32) * deviation * level
    return jnp.minimum(jnp.maximum(entries, -limit), limit).astype(kind)


def setup_inputs(seed: int = 0) -> dict:
    seeds = jax.random.split(jax.random.key(seed), 8)
    return {
        "pattern": normal_values(seeds[0], (2, NBX, NBY, NTH1, NPH1), 1.0, 6.0, ((1, 8), (3, 4))),
        "occupied": draw_occupied(jax.random.fold_in(seeds[7], 71), 0),
        "trans_fine": normal_values(seeds[2], (2, FAR, NTH1, NPH1), 27 ** -0.5, 1.25, ((2, 4),)),
        "trans_coarse": normal_values(seeds[3], (2, FAR, NTH2, NPH2), 27 ** -0.5, 1.25, ((2, 4),)),
        "theta_weights": jnp.clip(-0.19921875 + 0.99609375 * jax.random.uniform(seeds[4], (NTH2, 4), jnp.float32) ** block_levels(seeds[4], (NTH2, 4), ((0, 4),), -0.2, 0.2), -0.19921875, 0.796875).astype(jnp.bfloat16),
        "phi_matrix": normal_values(seeds[5], (NPH1, NPH2), NPH1 ** -0.5, 0.375),
        "child_phase": jnp.clip(jax.random.uniform(seeds[6], (4, NTH2, NPH2), jnp.float32, -3.140625, 3.140625), -3.140625, 3.140625),
    }


far_offsets = [(step_row, step_col) for step_row in range(-3, 4) for step_col in range(-3, 4) if max(abs(step_row), abs(step_col)) >= 2]


def allowed(parity, step):
    if step == 3:
        return 1.0 - parity
    if step == -3:
        return parity
    return jnp.ones_like(parity)


def translate(extended, table, occupied_dest, first_row):
    count_rows = extended.shape[1] - 6
    count_cols = extended.shape[2]
    padded = jnp.pad(extended, ((0, 0), (0, 0), (3, 3), (0, 0), (0, 0)))
    row_parity = ((first_row + jnp.arange(count_rows, dtype=jnp.int32)) % 2).astype(jnp.float32)
    col_parity = (jnp.arange(count_cols, dtype=jnp.int32) % 2).astype(jnp.float32)
    shape = (count_rows, count_cols, extended.shape[3], extended.shape[4])
    real_sum = jnp.zeros(shape, jnp.float32)
    imag_sum = jnp.zeros(shape, jnp.float32)
    for offset_code, (step_row, step_col) in enumerate(far_offsets):
        weight = allowed(row_parity, step_row)[:, None] * allowed(col_parity, step_col)[None, :]
        weight = weight[:, :, None, None]
        source = padded[:, 3 + step_row:3 + step_row + count_rows, 3 + step_col:3 + step_col + count_cols].astype(jnp.float32)
        factor_real = table[0, offset_code].astype(jnp.float32)
        factor_imag = table[1, offset_code].astype(jnp.float32)
        real_sum = real_sum + weight * (source[0] * factor_real - source[1] * factor_imag)
        imag_sum = imag_sum + weight * (source[0] * factor_imag + source[1] * factor_real)
    dest = occupied_dest.astype(jnp.float32)[:, :, None, None]
    return jnp.stack([real_sum * dest, imag_sum * dest])


def blocked_translate(source, table, occupied_dest, block):
    padded_rows = jnp.pad(source, ((0, 0), (3, 3), (0, 0), (0, 0), (0, 0)))
    count = source.shape[1] // block

    def one_block(index):
        start = (index * block).astype(jnp.int32)
        slab = lax.dynamic_slice_in_dim(padded_rows, start, block + 6, 1)
        dest = lax.dynamic_slice_in_dim(occupied_dest, start, block, 0)
        return translate(slab, table, dest, start).astype(jnp.bfloat16)

    result = lax.map(one_block, jnp.arange(count, dtype=jnp.int32))
    result = jnp.moveaxis(result, 0, 1)
    return result.reshape(2, count * block, source.shape[2], source.shape[3], source.shape[4])


def band_matrix(weights, columns):
    rows_count = weights.shape[0]
    row_ids = jnp.arange(rows_count, dtype=jnp.int32)[:, None]
    col_ids = jnp.arange(columns, dtype=jnp.int32)[None, :]
    band = jnp.zeros((rows_count, columns), jnp.float32)
    for stencil in range(4):
        band = band + jnp.where(col_ids == row_ids // 2 + 1 + stencil, weights[:, stencil:stencil + 1].astype(jnp.float32), 0.0)
    return band


def aggregate_block(slab, band, phi_matrix, phase_cos, phase_sin):
    theta_part = jnp.einsum('rc,xijcp->xijrp', band, slab.astype(jnp.float32)).astype(jnp.bfloat16)
    count_rows, count_cols = slab.shape[1], slab.shape[2]
    theta_rows, azimuths = band.shape[0], phi_matrix.shape[1]
    full = jnp.dot(theta_part.reshape(-1, phi_matrix.shape[0]), phi_matrix, preferred_element_type=jnp.float32)
    full = full.reshape(2, count_rows // 2, 2, count_cols // 2, 2, theta_rows, azimuths)
    real_part = jnp.sum(phase_cos * full[0] - phase_sin * full[1], axis=(1, 3))
    imag_part = jnp.sum(phase_cos * full[1] + phase_sin * full[0], axis=(1, 3))
    return jnp.stack([real_part, imag_part]).astype(jnp.bfloat16)


def reference(pattern, occupied, trans_fine, trans_coarse, theta_weights, phi_matrix, child_phase):
    masked = pattern * occupied.astype(jnp.bfloat16)[None, :, :, None, None]
    local_fine = blocked_translate(masked, trans_fine, occupied, RX)
    theta_padded = jnp.pad(masked, ((0, 0), (0, 0), (0, 0), (2, 2), (0, 0)))
    band = band_matrix(theta_weights, theta_padded.shape[3])
    phase_cos = jnp.cos(child_phase).reshape(2, 2, NTH2, NPH2)[None, :, None, :, :, :]
    phase_sin = jnp.sin(child_phase).reshape(2, 2, NTH2, NPH2)[None, :, None, :, :, :]
    count = NBX // RX

    def one_block(index):
        start = (index * RX).astype(jnp.int32)
        slab = lax.dynamic_slice_in_dim(theta_padded, start, RX, 1)
        return aggregate_block(slab, band, phi_matrix, phase_cos, phase_sin)

    coarse = lax.map(one_block, jnp.arange(count, dtype=jnp.int32))
    coarse = jnp.moveaxis(coarse, 0, 1).reshape(2, NBX // 2, NBY // 2, NTH2, NPH2)
    occupied_coarse = jnp.max(occupied.reshape(NBX // 2, 2, NBY // 2, 2), axis=(1, 3))
    local_coarse = blocked_translate(coarse, trans_coarse, occupied_coarse, RX // 2)
    return local_fine, local_coarse
```

```python
import functools

import jax
import jax.numpy as jnp
from jax import lax
from jax.experimental import pallas as pl
from jax.experimental.pallas import tpu as pltpu
from jax.sharding import PartitionSpec as P

far_offsets = [
    (step_row, step_col)
    for step_row in range(-3, 4)
    for step_col in range(-3, 4)
    if max(abs(step_row), abs(step_col)) >= 2
]
code_of = {step: code for code, step in enumerate(far_offsets)}
LANES = 128
VMEM_BYTES = 48 * 2**20


def steps_of(parity):
    return range(-3, 3) if parity else range(-2, 4)


def halo(masked):
    size = lax.axis_size("dir")
    up = [(i, i + 1) for i in range(size - 1)]
    down = [(j, i) for i, j in up]
    before = lax.ppermute(masked[:, :, :, -2:], "dir", up)
    after = lax.ppermute(masked[:, :, :, :2], "dir", down)
    return jnp.concatenate([before, after], axis=3)


def bands(theta_weights, rows, group):
    theta_rows = theta_weights.shape[0]
    row_ids = jnp.arange(theta_rows, dtype=jnp.int32)[:, None]
    col_ids = jnp.arange(rows + 4, dtype=jnp.int32)[None, :]
    band = jnp.zeros((theta_rows, rows + 4), jnp.float32)
    for stencil in range(4):
        band = band + jnp.where(
            col_ids == row_ids // 2 + 1 + stencil,
            theta_weights[:, stencil : stencil + 1].astype(jnp.float32),
            0.0,
        )
    band = band.astype(jnp.bfloat16)
    inner = band[:, 2 : rows + 2]
    outer = jnp.concatenate([band[:, :2], band[:, rows + 2 :]], axis=1)
    outer = jnp.stack(
        [jnp.pad(outer, ((0, 0), (4 * c, 4 * (group - 1 - c)))) for c in range(group)]
    )
    return inner, outer


def aggregate_kernel(m_ref, h_ref, inner_ref, outer_ref, phi_ref, cos_ref, sin_ref, out_ref):
    theta_rows = inner_ref.shape[0]
    real_sum = None
    for a in range(2):
        for b in range(2):
            parts = []
            for x in range(2):
                part = jnp.dot(inner_ref[...], m_ref[x, a, b], preferred_element_type=jnp.float32)
                part = part + jnp.dot(outer_ref[b], h_ref[x, a], preferred_element_type=jnp.float32)
                parts.append(part.astype(jnp.bfloat16))
            full = jnp.dot(
                jnp.concatenate(parts, axis=0), phi_ref[...], preferred_element_type=jnp.float32
            )
            full_real, full_imag = full[:theta_rows], full[theta_rows:]
            phase_cos, phase_sin = cos_ref[2 * a + b], sin_ref[2 * a + b]
            real = phase_cos * full_real - phase_sin * full_imag
            imag = phase_cos * full_imag + phase_sin * full_real
            real_sum, imag_sum = (real, imag) if real_sum is None else (real_sum + real, imag_sum + imag)
    out_ref[0, 0, 0] = real_sum.astype(jnp.bfloat16)
    out_ref[1, 0, 0] = imag_sum.astype(jnp.bfloat16)


def aggregate(chunk, halos, index, inner, outer, phi_matrix, phase_cos, phase_sin):
    _, rows, cols, polar, azimuths = chunk.shape
    theta_rows, fine = inner.shape[0], phi_matrix.shape[1]
    boxes = rows * cols
    flops = 2 * 2 * boxes * theta_rows * azimuths * (fine + polar) + boxes * theta_rows * fine * 8
    return pl.pallas_call(
        aggregate_kernel,
        grid=(rows // 2, cols // 2),
        in_specs=[
            pl.BlockSpec((2, 2, 2, polar, azimuths), lambda i, j: (0, i, j, 0, 0)),
            pl.BlockSpec((2, 2, 4 * cols, azimuths), lambda i, j: (0, i, index, 0)),
            pl.BlockSpec((theta_rows, polar), lambda i, j: (0, 0)),
            pl.BlockSpec((2, theta_rows, 4 * cols), lambda i, j: (j, 0, 0)),
            pl.BlockSpec((azimuths, fine), lambda i, j: (0, 0)),
            pl.BlockSpec((4, theta_rows, fine), lambda i, j: (0, 0, 0)),
            pl.BlockSpec((4, theta_rows, fine), lambda i, j: (0, 0, 0)),
        ],
        out_specs=pl.BlockSpec((2, 1, 1, theta_rows, fine), lambda i, j: (0, i, j, 0, 0)),
        out_shape=jax.ShapeDtypeStruct((2, rows // 2, cols // 2, theta_rows, fine), jnp.bfloat16),
        compiler_params=pltpu.CompilerParams(vmem_limit_bytes=VMEM_BYTES),
        cost_estimate=pl.CostEstimate(
            flops=flops, bytes_accessed=4 * 2**20, transcendentals=0
        ),
    )(chunk, halos, inner, outer, phi_matrix, phase_cos, phase_sin)


def translate_kernel(plan, odd_ref, dest_ref, *refs):
    pieces, first, last, columns, rows = plan
    count = len(pieces)
    own_refs, swap_refs, far_refs = refs[:count], refs[count : 2 * count], refs[2 * count : 3 * count]
    table_ref, out_ref, source_ref, factor_ref, sum_ref = refs[3 * count :]
    polar, azimuths = table_ref.shape[2], table_ref.shape[3]
    half = min(8, polar)
    even = odd_ref[0] == 0
    width = last - first + 4
    f32 = jnp.float32

    for col in range(width):
        if not 0 <= first - 2 + col < columns:
            for row in range(rows + 4):
                for form in range(3):
                    source_ref[row, col, form] = jnp.zeros((polar, LANES), f32)

    def keep(row, col, real, imag):
        real, imag = real.astype(f32), imag.astype(f32)
        source_ref[row, col, 0] = real
        source_ref[row, col, 1] = imag
        source_ref[row, col, 2] = real + imag

    def tile(index, carry):
        lanes = pl.ds(pl.multiple_of(index * LANES, LANES), LANES)
        for piece, (start, stop) in enumerate(pieces):
            for col in range(max(start, first - 2), min(stop, last + 2)):
                at, to = col - start, col - (first - 2)
                for row in range(rows):
                    keep(row + 2, to, *[own_refs[piece][x, row, at, :, lanes] for x in range(2)])
                for row in range(2):
                    swap = [swap_refs[piece][x, row, at, :, lanes] for x in range(2)]
                    far = [far_refs[piece][x, row, at, :, lanes] for x in range(2)]
                    keep(row, to, *[jnp.where(even, far[x], swap[x]) for x in range(2)])
                    keep(rows + 2 + row, to, *[jnp.where(even, swap[x], far[x]) for x in range(2)])
        for code in range(len(far_offsets)):
            real = table_ref[0, code, :, lanes].astype(f32)
            imag = table_ref[1, code, :, lanes].astype(f32)
            factor_ref[code, 0] = real
            factor_ref[code, 1] = imag - real
            factor_ref[code, 2] = imag + real

        def part(which, carry):
            subs = pl.ds(pl.multiple_of(which * half, half), half)
            for row in range(rows):
                sums = [None] * (last - first)
                for step_row in steps_of(row % 2):
                    found = {}
                    for step_col in range(-3, 4):
                        if (step_row, step_col) not in code_of:
                            continue
                        code = code_of[step_row, step_col]
                        factor = [factor_ref[code, form, subs] for form in range(3)]
                        for dest in range(last - first):
                            if step_col not in steps_of((first + dest) % 2):
                                continue
                            col = dest + 2 + step_col
                            if col not in found:
                                found[col] = [
                                    source_ref[row + 2 + step_row, col, form, subs] for form in range(3)
                                ]
                            real, imag, both = found[col]
                            terms = (both * factor[0], real * factor[1], imag * factor[2])
                            sums[dest] = (
                                terms
                                if sums[dest] is None
                                else [s + t for s, t in zip(sums[dest], terms)]
                            )
                for dest in range(last - first):
                    shared, cross, other = sums[dest]
                    flag = dest_ref[row, first + dest].astype(f32)
                    sum_ref[0, row, dest, subs] = (shared - other) * flag
                    sum_ref[1, row, dest, subs] = (shared + cross) * flag
            return carry

        lax.fori_loop(0, polar // half, part, 0)
        for x in range(2):
            for row in range(rows):
                for dest in range(last - first):
                    out_ref[x, row, dest, :, lanes] = sum_ref[x, row, dest].astype(jnp.bfloat16)
        return carry

    lax.fori_loop(0, azimuths // LANES, tile, 0)


def translate(own, swap, far, starts, table, dest, odd, first, last):
    rows, polar, azimuths = own[0].shape[1], table.shape[2], table.shape[3]
    columns = starts[-1]
    used = [
        k for k in range(len(own)) if starts[k] < last + 2 and starts[k + 1] > first - 2
    ]
    pieces = [(starts[k], starts[k + 1]) for k in used]
    block = min(16, polar)
    edge = rows // 2 - 1
    own_specs = [
        pl.BlockSpec((2, rows, stop - start, block, azimuths), lambda t, odd, dest: (0, 0, 0, t, 0))
        for start, stop in pieces
    ]
    swap_specs = [
        pl.BlockSpec(
            (2, 2, stop - start, block, azimuths), lambda t, odd, dest: (0, odd[0] * edge, 0, t, 0)
        )
        for start, stop in pieces
    ]
    far_specs = [
        pl.BlockSpec(
            (2, 2, stop - start, block, azimuths),
            lambda t, odd, dest: (0, (1 - odd[0]) * edge, 0, t, 0),
        )
        for start, stop in pieces
    ]
    table_spec = pl.BlockSpec((2, len(far_offsets), block, azimuths), lambda t, odd, dest: (0, 0, t, 0))
    wide = last - first
    return pl.pallas_call(
        functools.partial(translate_kernel, (pieces, first, last, columns, rows)),
        grid_spec=pltpu.PrefetchScalarGridSpec(
            num_scalar_prefetch=2,
            grid=(polar // block,),
            in_specs=[*own_specs, *swap_specs, *far_specs, table_spec],
            out_specs=pl.BlockSpec(
                (2, rows, wide, block, azimuths), lambda t, odd, dest: (0, 0, 0, t, 0)
            ),
            scratch_shapes=[
                pltpu.VMEM((rows + 4, wide + 4, 3, block, LANES), jnp.float32),
                pltpu.VMEM((len(far_offsets), 3, block, LANES), jnp.float32),
                pltpu.VMEM((2, rows, wide, block, LANES), jnp.float32),
            ],
        ),
        out_shape=jax.ShapeDtypeStruct((2, rows, wide, polar, azimuths), jnp.bfloat16),
        compiler_params=pltpu.CompilerParams(vmem_limit_bytes=VMEM_BYTES),
        cost_estimate=pl.CostEstimate(
            flops=rows * wide * polar * azimuths * 27 * 8,
            bytes_accessed=8 * 2**20,
            transcendentals=0,
        ),
    )(odd, dest, *[own[k] for k in used], *[swap[k] for k in used], *[far[k] for k in used], table)


def local(pattern, occupied, trans_fine, trans_coarse, theta_weights, phi_matrix, child_phase):
    _, count_rows, count_cols, polar, azimuths = pattern.shape
    groups = lax.axis_size("box")
    group = lax.axis_index("box")
    odd = (group % 2).astype(jnp.int32).reshape(1)
    partner = [(i, i ^ 1) for i in range(groups)]
    onward = [(i, i + 2) for i in range(0, groups - 2, 2)] + [(i, i - 2) for i in range(3, groups, 2)]
    chunks = 4
    width = count_cols // chunks
    starts = [k * width for k in range(chunks + 1)]
    coarse_starts = [k * width // 2 for k in range(chunks + 1)]

    flags = occupied.astype(jnp.bfloat16)[None, :, :, None, None]
    own = [
        pattern[:, :, starts[k] : starts[k + 1]] * flags[:, :, starts[k] : starts[k + 1]]
        for k in range(chunks)
    ]
    edges = jnp.concatenate([pattern[:, :, :, :2], pattern[:, :, :, -2:]], axis=3) * flags
    own_halo = halo(edges).reshape(2, count_rows, -1, polar, azimuths)
    extra = own_halo.shape[2]
    swap, far = [], []
    for k in range(chunks):
        sent = jnp.concatenate([own[k], own_halo], axis=2) if k == 1 else own[k]
        got = lax.ppermute(sent, "box", partner)
        swap.append(got)
        far.append(lax.ppermute(got, "box", onward))
    halos = []
    for held in (own_halo, swap[1][:, :, width:], far[1][:, :, width:]):
        halos.append(held.reshape(2, count_rows, extra * polar, azimuths))
    swap[1], far[1] = swap[1][:, :, :width], far[1][:, :, :width]

    inner, outer = bands(theta_weights, polar, width)
    phase_cos, phase_sin = jnp.cos(child_phase), jnp.sin(child_phase)
    coarse = [
        [
            aggregate(held[k], halos[which], k, inner, outer, phi_matrix, phase_cos, phase_sin)
            for k in range(chunks)
        ]
        for which, held in enumerate((own, swap, far))
    ]
    occupied_coarse = jnp.max(occupied.reshape(count_rows // 2, 2, count_cols // 2, 2), axis=(1, 3))

    cuts = [0, starts[2] - 2, starts[3] - 2, count_cols]
    fine = [
        translate(own, swap, far, starts, trans_fine, occupied, odd, cuts[k], cuts[k + 1])
        for k in range(3)
    ]
    cuts = [0, coarse_starts[2], coarse_starts[4]]
    coarser = [
        translate(*coarse, coarse_starts, trans_coarse, occupied_coarse, odd, cuts[k], cuts[k + 1])
        for k in range(2)
    ]
    return jnp.concatenate(fine, axis=2), jnp.concatenate(coarser, axis=2)


def solution(mesh):
    return jax.shard_map(
        local,
        mesh=mesh,
        in_specs=(
            P(None, "box", None, "dir", None),
            P("box", None),
            P(None, None, "dir", None),
            P(None, None, "dir", None),
            P("dir", None),
            P(),
            P(None, "dir", None),
        ),
        out_specs=(P(None, "box", None, "dir", None), P(None, "box", None, "dir", None)),
        check_vma=False,
    )
```

```python
import functools

import jax
import jax.numpy as jnp
from jax import lax
from jax.experimental import pallas as pl
from jax.experimental.pallas import tpu as pltpu
from jax.sharding import PartitionSpec as P

far_offsets = [
    (step_row, step_col)
    for step_row in range(-3, 4)
    for step_col in range(-3, 4)
    if max(abs(step_row), abs(step_col)) >= 2
]
code_of = {step: code for code, step in enumerate(far_offsets)}
LANES = 128
VMEM_BYTES = 48 * 2**20


def steps_of(parity):
    return range(-3, 3) if parity else range(-2, 4)


def halo(masked):
    size = lax.axis_size("dir")
    up = [(i, i + 1) for i in range(size - 1)]
    down = [(j, i) for i, j in up]
    before = lax.ppermute(masked[:, :, :, -2:], "dir", up)
    after = lax.ppermute(masked[:, :, :, :2], "dir", down)
    return jnp.concatenate([before, after], axis=3)


def bands(theta_weights, rows, group):
    theta_rows = theta_weights.shape[0]
    row_ids = jnp.arange(theta_rows, dtype=jnp.int32)[:, None]
    col_ids = jnp.arange(rows + 4, dtype=jnp.int32)[None, :]
    band = jnp.zeros((theta_rows, rows + 4), jnp.float32)
    for stencil in range(4):
        band = band + jnp.where(
            col_ids == row_ids // 2 + 1 + stencil,
            theta_weights[:, stencil : stencil + 1].astype(jnp.float32),
            0.0,
        )
    band = band.astype(jnp.bfloat16)
    inner = band[:, 2 : rows + 2]
    outer = jnp.concatenate([band[:, :2], band[:, rows + 2 :]], axis=1)
    outer = jnp.stack(
        [jnp.pad(outer, ((0, 0), (4 * c, 4 * (group - 1 - c)))) for c in range(group)]
    )
    return inner, outer


def cost(us):
    return pl.CostEstimate(flops=0, bytes_accessed=int(us * 3.3e5), transcendentals=0)


def aggregate_kernel(masked, group, pieces, *refs):
    refs = list(refs)
    flag_ref = refs.pop(0) if masked else None
    m_refs = [refs.pop(0) for _ in range(pieces)]
    h_ref, inner_ref, outer_ref, phi_ref, cos_ref, sin_ref, out_ref, part_ref, full_ref = refs
    theta_rows, polar = inner_ref.shape
    boxes = out_ref.shape[2]
    span = 2 * boxes // pieces
    azimuths, fine = phi_ref.shape
    f32, bf16 = jnp.float32, jnp.bfloat16
    pairs = [(x, a) for x in range(2) for a in range(2)]
    for col in range(2 * boxes):
        blocks = [m_refs[col // span][x, a, col % span] for x, a in pairs]
        if masked:
            row, at = 2 * pl.program_id(0), 2 * boxes * pl.program_id(1) + col
            flags = [flag_ref[row + a, at].astype(f32).astype(bf16) for x, a in pairs]
            blocks = [block * flag for block, flag in zip(blocks, flags)]
        own = jnp.concatenate(blocks, axis=1)
        rows = pl.ds(col // group * 4 * group, 4 * group)
        beside = jnp.concatenate([h_ref[x, a, rows] for x, a in pairs], axis=1)
        outer = outer_ref[col % group]
        if polar % 16 == 0:
            both = jnp.concatenate([inner_ref[...], outer], axis=1)
            part = jnp.dot(both, jnp.concatenate([own, beside], axis=0), preferred_element_type=f32)
        else:
            part = jnp.dot(inner_ref[...], own, preferred_element_type=f32)
            part = part + jnp.dot(outer, beside, preferred_element_type=f32)
        part = part.astype(bf16)
        for n, (x, a) in enumerate(pairs):
            slot = ((col // 2) * 4 + 2 * a + col % 2) * 2 + x
            part_ref[pl.ds(slot * theta_rows, theta_rows), :] = part[:, n * azimuths : (n + 1) * azimuths]
    full = jnp.dot(part_ref[...], phi_ref[...], preferred_element_type=f32)
    full_ref[...] = full.reshape(full_ref.shape)
    tiles = fine // LANES

    def combine(index, carry):
        start = pl.multiple_of((index // tiles) * 16, 16)
        subs = pl.ds(start, 16)
        lanes = pl.ds(pl.multiple_of((index % tiles) * LANES, LANES), LANES)
        phases = [(cos_ref[k, subs, lanes], sin_ref[k, subs, lanes]) for k in range(4)]
        for box in range(boxes):
            real_sum = None
            for k, (phase_cos, phase_sin) in enumerate(phases):
                real, imag = [full_ref[8 * box + 2 * k + x, subs, lanes] for x in range(2)]
                terms = (phase_cos * real - phase_sin * imag, phase_cos * imag + phase_sin * real)
                if real_sum is None:
                    real_sum, imag_sum = terms
                else:
                    real_sum, imag_sum = real_sum + terms[0], imag_sum + terms[1]
            out_ref[0, 0, box, subs, lanes] = real_sum.astype(bf16)
            out_ref[1, 0, box, subs, lanes] = imag_sum.astype(bf16)
        return carry

    lax.fori_loop(0, (theta_rows // 16) * tiles, combine, 0)


def aggregate(held, cols, halos, index, inner, outer, phi_matrix, phase_cos, phase_sin, flags=None):
    _, rows, _, polar, azimuths = held[0].shape
    theta_rows, fine = inner.shape[0], phi_matrix.shape[1]
    group = outer.shape[0]
    pieces = len(held)
    total = cols * pieces
    masked = flags is not None
    return pl.pallas_call(
        functools.partial(aggregate_kernel, masked, group, pieces),
        grid=(rows // 2, 1),
        in_specs=[pl.BlockSpec(memory_space=pltpu.SMEM)] * masked
        + [pl.BlockSpec((2, 2, cols, polar, azimuths), lambda i, j: (0, i, 0, 0, 0))] * pieces
        + [
            pl.BlockSpec((2, 2, 4 * total, azimuths), lambda i, j: (0, i, index, 0)),
            pl.BlockSpec((theta_rows, polar), lambda i, j: (0, 0)),
            pl.BlockSpec((group, theta_rows, 4 * group), lambda i, j: (0, 0, 0)),
            pl.BlockSpec((azimuths, fine), lambda i, j: (0, 0)),
            pl.BlockSpec((4, theta_rows, fine), lambda i, j: (0, 0, 0)),
            pl.BlockSpec((4, theta_rows, fine), lambda i, j: (0, 0, 0)),
        ],
        out_specs=pl.BlockSpec((2, 1, total // 2, theta_rows, fine), lambda i, j: (0, i, 0, 0, 0)),
        out_shape=jax.ShapeDtypeStruct((2, rows // 2, total // 2, theta_rows, fine), jnp.bfloat16),
        scratch_shapes=[
            pltpu.VMEM((4 * total * theta_rows, azimuths), jnp.bfloat16),
            pltpu.VMEM((4 * total, theta_rows, fine), jnp.float32),
        ],
        compiler_params=pltpu.CompilerParams(vmem_limit_bytes=VMEM_BYTES),
        cost_estimate=cost(0.5 * rows * total / 4 + 1),
    )(*[flags] * masked, *held, halos, inner, outer, phi_matrix, phase_cos, phase_sin)


def runs_of(row, rows, own, sides):
    steps = [
        step
        for step in steps_of(row % 2)
        if (own if 0 <= row + step < rows else sides)
    ]
    runs = []
    for step in steps:
        kind = (abs(step) >= 2, step > 0 and abs(step) >= 2)
        if runs and runs[-1][0] == kind and runs[-1][2] == step:
            runs[-1][2] = step + 1
        else:
            runs.append([kind, step, step + 1])
    return [(kind[0], start, stop) for kind, start, stop in runs]


def translate_kernel(plan, odd_ref, dest_ref, *refs):
    own_pieces, swap_pieces, far_pieces, first, last, columns, rows, partial, final, whole = plan
    refs = list(refs)
    own_refs = [refs.pop(0) for _ in own_pieces]
    swap_refs = [refs.pop(0) for _ in swap_pieces]
    far_refs = [refs.pop(0) for _ in far_pieces]
    table_ref = refs.pop(0)
    partial_ref = refs.pop(0) if partial else None
    if whole:
        refs.pop(0)
    out_ref = refs.pop(0)
    source_ref, factor_ref = refs.pop(0), refs.pop(0)
    sum_ref = refs.pop(0) if final else None
    polar, azimuths = table_ref.shape[2], table_ref.shape[3]
    half = min(8, polar)
    even = odd_ref[0] == 0
    wide = last - first
    span = wide + 4
    f32 = jnp.float32
    at_once = 8 if wide % 8 == 0 else wide

    zero = jnp.zeros((polar, LANES), f32)

    def clear(row, carry):
        for col in range(span):
            if not 0 <= first - 2 + col < columns:
                for form in range(3):
                    source_ref[form, row, col] = zero
        return carry

    lax.fori_loop(0, rows + 4, clear, 0)

    def keep(row, col, real, imag, flag=None):
        real, imag = real.astype(f32), imag.astype(f32)
        if flag is not None:
            real, imag = real * flag, imag * flag
        source_ref[0, row, col] = real
        source_ref[1, row, col] = imag
        source_ref[2, row, col] = real + imag

    def tile(index, carry):
        lanes = pl.ds(pl.multiple_of(index * LANES, LANES), LANES)

        def keep_own(row, carry):
            for piece, (start, stop, raw) in enumerate(own_pieces):
                for col in range(max(start, first - 2), min(stop, last + 2)):
                    flag = dest_ref[row, col].astype(f32) if raw else None
                    keep(row + 2, col - (first - 2), *[own_refs[piece][x, row, col - start, :, lanes] for x in range(2)], flag)
            return carry

        def keep_sides(row, carry):
            def load(pieces, piece_refs, col):
                ref, at = [
                    (ref, col - start) for ref, (start, stop) in zip(piece_refs, pieces) if start <= col < stop
                ][0]
                return [ref[x, row, at, :, lanes] for x in range(2)]

            for col in range(max(0, first - 2), min(columns, last + 2)):
                swap, far = load(swap_pieces, swap_refs, col), load(far_pieces, far_refs, col)
                to = col - (first - 2)
                keep(row, to, *[jnp.where(even, far[x], swap[x]) for x in range(2)])
                keep(rows + 2 + row, to, *[jnp.where(even, swap[x], far[x]) for x in range(2)])
            return carry

        if own_pieces:
            lax.fori_loop(0, rows, keep_own, 0)
        if swap_pieces:
            lax.fori_loop(0, 2, keep_sides, 0)

        def keep_factors(block, carry):
            for code in [block * 4 + n for n in range(4)]:
                real = table_ref[0, code, :, lanes].astype(f32)
                imag = table_ref[1, code, :, lanes].astype(f32)
                factor_ref[0, code] = real
                factor_ref[1, code] = imag - real
                factor_ref[2, code] = imag + real
            return carry

        lax.fori_loop(0, len(far_offsets) // 4, keep_factors, 0)

        def part(index, carry):
            subs = pl.ds(pl.multiple_of((index % (polar // half)) * half, half), half)
            begin = (index // (polar // half)) * at_once
            for row in range(rows):

                def one_step(far_row, base, start, row=row):
                    cols = [q for q in range(-3, 4) if far_row or abs(q) >= 2]

                    def body(step, sums):
                        sums = [list(s) for s in sums]
                        found = {}
                        code = base + step * len(cols)
                        for n, step_col in enumerate(cols):
                            factor = [factor_ref[form, code + n, subs] for form in range(3)]
                            for dest in range(at_once):
                                if step_col not in steps_of(dest % 2):
                                    continue
                                col = dest + 2 + step_col
                                if col not in found:
                                    found[col] = [
                                        source_ref[form, row + 2 + start + step, begin + col, subs]
                                        for form in range(3)
                                    ]
                                real, imag, both = found[col]
                                terms = (both * factor[0], real * factor[1], imag * factor[2])
                                sums[dest] = [s + t for s, t in zip(sums[dest], terms)]
                        return tuple(tuple(s) for s in sums)

                    return body

                nothing = jnp.zeros((half, LANES), f32)
                sums = tuple((nothing,) * 3 for _ in range(at_once))
                for far_row, start, stop in runs_of(row, rows, bool(own_pieces), bool(swap_pieces)):
                    base = code_of[start, -3]
                    sums = lax.fori_loop(0, stop - start, one_step(far_row, base, start), sums)
                for dest in range(at_once):
                    shared, cross, other = sums[dest]
                    pair = [shared - other, shared + cross]
                    for x in range(2):
                        value = pair[x]
                        if partial:
                            value = value + partial_ref[x, row, begin + dest, subs, lanes]
                        if final:
                            flag = dest_ref[row, first + begin + dest].astype(f32)
                            sum_ref[x, row, begin + dest, subs] = value * flag
                        else:
                            out_ref[x, row, begin + dest, subs, lanes] = value
            return carry

        lax.fori_loop(0, (polar // half) * (wide // at_once), part, 0)

        def finish(row, carry):
            for x in range(2):
                for dest in range(wide):
                    out_ref[x, row, dest, :, lanes] = sum_ref[x, row, dest].astype(jnp.bfloat16)
            return carry

        if final:
            lax.fori_loop(0, rows, finish, 0)
        return carry

    lax.fori_loop(0, azimuths // LANES, tile, 0)


def translate(own, sides, table, dest, odd, first, last, partial=None, final=True, whole=None, raw=False, part=(0, 1)):
    rows, columns = dest.shape
    polar, azimuths = table.shape[2], table.shape[3]
    block = min(16, polar)
    edge = rows // 2 - 1
    wide = last - first
    steps = polar // block // part[1]
    skip = part[0] * steps

    own_pieces = [(0, columns, raw)] if own else []
    swap_side, far_side = [
        [chunk for chunk in side if chunk[1] < last + 2 and chunk[2] > first - 2] for side in sides or ([], [])
    ]
    at = first // wide
    operands = list(own)
    specs = [
        pl.BlockSpec((2, rows, stop - start, block, azimuths), lambda t, odd, dest: (0, 0, 0, t + skip, 0))
        for start, stop, _ in own_pieces
    ]
    for side, place in ((swap_side, lambda odd: odd), (far_side, lambda odd: 1 - odd)):
        operands += [held for held, start, stop in side]
        specs += [
            pl.BlockSpec(
                (2, 2, stop - start, block, azimuths),
                lambda t, odd, dest, place=place: (0, place(odd[0]) * edge, 0, t + skip, 0),
            )
            for held, start, stop in side
        ]
    operands.append(table)
    specs.append(pl.BlockSpec((2, len(far_offsets), block, azimuths), lambda t, odd, dest: (0, 0, t + skip, 0)))
    out_spec = pl.BlockSpec((2, rows, wide, block, azimuths), lambda t, odd, dest: (0, 0, at, t + skip, 0))
    if partial is not None:
        operands.append(partial)
        specs.append(out_spec)
    aliases = {}
    if whole is not None:
        operands.append(whole)
        specs.append(pl.BlockSpec(memory_space=pl.ANY))
        aliases = {len(operands) + 1: 0}
    kind = jnp.bfloat16 if final else jnp.float32
    scratch = [
        pltpu.VMEM((3, rows + 4, wide + 4, block, LANES), jnp.float32),
        pltpu.VMEM((3, len(far_offsets), block, LANES), jnp.float32),
    ]
    if final:
        scratch.append(pltpu.VMEM((2, rows, wide, block, LANES), jnp.float32))
    swap_pieces, far_pieces = [[chunk[1:] for chunk in side] for side in (swap_side, far_side)]
    plan = (own_pieces, swap_pieces, far_pieces, first, last, columns, rows, partial is not None, final, whole is not None)
    share = ((2 / 3 if rows > 2 else 2 / 9) if own else 0) + ((1 / 3 if rows > 2 else 7 / 9) if sides else 0)
    return pl.pallas_call(
        functools.partial(translate_kernel, plan),
        grid_spec=pltpu.PrefetchScalarGridSpec(
            num_scalar_prefetch=2,
            grid=(steps,),
            in_specs=specs,
            out_specs=out_spec,
            scratch_shapes=scratch,
        ),
        out_shape=jax.ShapeDtypeStruct((2, rows, columns, polar, azimuths), kind),
        input_output_aliases=aliases,
        compiler_params=pltpu.CompilerParams(vmem_limit_bytes=VMEM_BYTES),
        cost_estimate=cost(22 * share * wide / columns / part[1] + 1),
    )(odd, dest, *operands)


def local(pattern, occupied, trans_fine, trans_coarse, theta_weights, phi_matrix, child_phase):
    _, count_rows, count_cols, polar, azimuths = pattern.shape
    groups = lax.axis_size("box")
    group = lax.axis_index("box")
    odd = (group % 2).astype(jnp.int32).reshape(1)
    partner = [(i, i ^ 1) for i in range(groups)]
    onward = [(i, i + 2) for i in range(0, groups - 2, 2)] + [(i, i - 2) for i in range(3, groups, 2)]
    chunks = 4
    width = count_cols // chunks
    starts = [k * width for k in range(chunks + 1)]

    flags = occupied.astype(jnp.bfloat16)[None, :, :, None, None]

    def chunk(values, k):
        return values[:, :, starts[k] : starts[k + 1]] * flags[:, :, starts[k] : starts[k + 1]]

    def flat(held):
        return held.reshape(2, count_rows, -1, azimuths)

    def placed(held, cols):
        ends = [sum(cols[: k + 1]) for k in range(len(cols))]
        return [(value, end - size, end) for value, size, end in zip(held, cols, ends)]

    def send(value, pairs):
        return lax.ppermute(value, "box", pairs)

    def onto(held, index, halos):
        return aggregate(held, width, halos, index, *fixed)

    parts = 2 if polar >= 32 else 1
    fine_plan = (trans_fine, occupied, odd)

    own = [chunk(pattern, 0)]
    rest, own[0] = lax.optimization_barrier((pattern, own[0]))
    edges = jnp.concatenate([rest[:, :, :, :2], rest[:, :, :, -2:]], axis=3) * flags
    own += [chunk(rest, k) for k in range(1, chunks)]

    swap0 = send(own[0], partner)
    own_halo = halo(edges).reshape(2, count_rows, -1, polar, azimuths)
    fine_sums = translate([rest], None, *fine_plan, 0, count_cols, final=False, raw=True, part=(0, parts))
    phases = (jnp.cos(child_phase), jnp.sin(child_phase))
    swap0, own_halo, fine_sums, phases, own, rest = lax.optimization_barrier(
        (swap0, own_halo, fine_sums, phases, own, rest)
    )
    inner, outer = bands(theta_weights, polar, width)
    fixed = (inner, outer, phi_matrix, *phases)

    swap1 = send(jnp.concatenate([own[1], own_halo], axis=2), partner)
    far0 = send(swap0, onward)
    coarse_own = aggregate([rest], count_cols, flat(own_halo), 0, *fixed, flags=occupied)
    swap0, swap1, far0, coarse_own, fine_sums, own, rest = lax.optimization_barrier(
        (swap0, swap1, far0, coarse_own, fine_sums, own, rest)
    )

    swap2 = send(own[2], partner)
    far1 = send(swap1, onward)
    swap_halo = flat(swap1[:, :, width:])
    if parts > 1:
        fine_sums = translate(
            [rest], None, *fine_plan, 0, count_cols, final=False, raw=True, whole=fine_sums, part=(1, parts)
        )
    coarse_swap = [onto([swap0, swap1], 0, swap_halo)]
    swap2, far0, far1, coarse_swap, fine_sums, own, swap_halo = lax.optimization_barrier(
        (swap2, far0, far1, coarse_swap, fine_sums, own, swap_halo)
    )

    swap3 = send(own[3], partner)
    far2 = send(swap2, onward)
    far_halo = flat(far1[:, :, width:])
    coarse_far = [onto([far0, far1], 0, far_halo)]
    coarse_swap.append(onto([swap2], 2, swap_halo))
    swap3, far2, far_halo, coarse_far, coarse_swap, fine_sums, swap_halo = lax.optimization_barrier(
        (swap3, far2, far_halo, coarse_far, coarse_swap, fine_sums, swap_halo)
    )

    far3 = send(swap3, onward)
    swap, far = [swap0, swap1, swap2, swap3], [far0, far1, far2]
    half = count_cols // 2
    coarse_swap.append(onto([swap3], 3, swap_halo))
    coarse_far.append(onto([far2], 2, far_halo))
    fine_sides = [placed(swap, [width] * 4), placed(far, [width] * 3)]
    local_fine = translate([], fine_sides, *fine_plan, 0, half, partial=fine_sums)
    far3, coarse_far, coarse_swap, local_fine, fine_sums = lax.optimization_barrier(
        (far3, coarse_far, coarse_swap, local_fine, fine_sums)
    )

    coarse_far.append(onto([far3], 3, far_halo))
    occupied_coarse = jnp.max(occupied.reshape(count_rows // 2, 2, count_cols // 2, 2), axis=(1, 3))
    coarse_sides = [placed(held, [width, width // 2, width // 2]) for held in (coarse_swap, coarse_far)]
    local_coarse = translate([coarse_own], coarse_sides, trans_coarse, occupied_coarse, odd, 0, half)
    fine_sides = [placed(swap, [width] * 4), placed([*far, far3], [width] * 4)]
    local_fine = translate([], fine_sides, *fine_plan, half, count_cols, partial=fine_sums, whole=local_fine)
    return local_fine, local_coarse


def solution(mesh):
    return jax.shard_map(
        local,
        mesh=mesh,
        in_specs=(
            P(None, "box", None, "dir", None),
            P("box", None),
            P(None, None, "dir", None),
            P(None, None, "dir", None),
            P("dir", None),
            P(),
            P(None, "dir", None),
        ),
        out_specs=(P(None, "box", None, "dir", None), P(None, "box", None, "dir", None)),
        check_vma=False,
    )
```

```python
import functools

import jax
import jax.numpy as jnp
from jax import lax
from jax.experimental import pallas as pl
from jax.experimental.pallas import tpu as pltpu
from jax.sharding import PartitionSpec as P

far_offsets = [
    (step_row, step_col)
    for step_row in range(-3, 4)
    for step_col in range(-3, 4)
    if max(abs(step_row), abs(step_col)) >= 2
]
code_of = {step: code for code, step in enumerate(far_offsets)}
LANES = 128
VMEM_BYTES = 48 * 2**20


def steps_of(parity):
    return range(-3, 3) if parity else range(-2, 4)


def halo(masked):
    size = lax.axis_size("dir")
    up = [(i, i + 1) for i in range(size - 1)]
    down = [(j, i) for i, j in up]
    before = lax.ppermute(masked[:, :, :, -2:], "dir", up)
    after = lax.ppermute(masked[:, :, :, :2], "dir", down)
    return before, after


def bands(theta_weights, rows, group):
    theta_rows = theta_weights.shape[0]
    row_ids = jnp.arange(theta_rows, dtype=jnp.int32)[:, None]
    col_ids = jnp.arange(rows + 4, dtype=jnp.int32)[None, :]
    band = jnp.zeros((theta_rows, rows + 4), jnp.float32)
    for stencil in range(4):
        band = band + jnp.where(
            col_ids == row_ids // 2 + 1 + stencil,
            theta_weights[:, stencil : stencil + 1].astype(jnp.float32),
            0.0,
        )
    band = band.astype(jnp.bfloat16)
    inner = band[:, 2 : rows + 2]
    outer = jnp.concatenate([band[:, :2], band[:, rows + 2 :]], axis=1)
    outer = jnp.stack(
        [jnp.pad(outer, ((0, 0), (4 * c, 4 * (group - 1 - c)))) for c in range(group)]
    )
    return inner, outer


def cost(us):
    return pl.CostEstimate(flops=0, bytes_accessed=int(us * 3.3e5), transcendentals=0)


def mask_kernel(flag_ref, pattern_ref, out_ref):
    for row in range(out_ref.shape[1]):
        for col in range(out_ref.shape[2]):
            flag = flag_ref[row, col].astype(jnp.float32).astype(jnp.bfloat16)
            for x in range(2):
                out_ref[x, row, col] = pattern_ref[x, row, col] * flag


def mask_first(pattern, occupied, width):
    _, rows, _, polar, azimuths = pattern.shape
    shape = (2, rows, width, polar, azimuths)
    spec = pl.BlockSpec(shape, lambda i: (0, 0, 0, 0, 0))
    return pl.pallas_call(
        mask_kernel,
        grid=(1,),
        in_specs=[pl.BlockSpec(memory_space=pltpu.SMEM), spec],
        out_specs=spec,
        out_shape=jax.ShapeDtypeStruct(shape, jnp.bfloat16),
        compiler_params=pltpu.CompilerParams(vmem_limit_bytes=60 * 2**20),
        cost_estimate=cost(1),
    )(occupied, pattern)


def aggregate_kernel(masked, group, widths, *refs):
    refs = list(refs)
    flag_ref = refs.pop(0) if masked else None
    m_refs = [refs.pop(0) for _ in widths]
    columns = [(ref, at) for ref, width in zip(m_refs, widths) for at in range(width)]
    h_ref, inner_ref, outer_ref, phi_ref, cos_ref, sin_ref, out_ref, part_ref, full_ref = refs
    theta_rows, polar = inner_ref.shape
    boxes = out_ref.shape[2]
    azimuths, fine = phi_ref.shape
    f32, bf16 = jnp.float32, jnp.bfloat16
    pairs = [(x, a) for x in range(2) for a in range(2)]
    for col in range(2 * boxes):
        ref, column = columns[col]
        blocks = [ref[x, a, column] for x, a in pairs]
        if masked:
            row, at = 2 * pl.program_id(0), 2 * boxes * pl.program_id(1) + col
            flags = [flag_ref[row + a, at].astype(f32).astype(bf16) for x, a in pairs]
            blocks = [block * flag for block, flag in zip(blocks, flags)]
        own = jnp.concatenate(blocks, axis=1)
        rows = pl.ds(col // group * 4 * group, 4 * group)
        beside = jnp.concatenate([h_ref[x, a, rows] for x, a in pairs], axis=1)
        outer = outer_ref[col % group]
        if polar % 16 == 0:
            both = jnp.concatenate([inner_ref[...], outer], axis=1)
            part = jnp.dot(both, jnp.concatenate([own, beside], axis=0), preferred_element_type=f32)
        else:
            part = jnp.dot(inner_ref[...], own, preferred_element_type=f32)
            part = part + jnp.dot(outer, beside, preferred_element_type=f32)
        part = part.astype(bf16)
        for n, (x, a) in enumerate(pairs):
            slot = ((col // 2) * 4 + 2 * a + col % 2) * 2 + x
            part_ref[pl.ds(slot * theta_rows, theta_rows), :] = part[:, n * azimuths : (n + 1) * azimuths]
    full = jnp.dot(part_ref[...], phi_ref[...], preferred_element_type=f32)
    full_ref[...] = full.reshape(full_ref.shape)
    tiles = fine // LANES

    def combine(index, carry):
        start = pl.multiple_of((index // tiles) * 16, 16)
        subs = pl.ds(start, 16)
        lanes = pl.ds(pl.multiple_of((index % tiles) * LANES, LANES), LANES)
        phases = [(cos_ref[k, subs, lanes], sin_ref[k, subs, lanes]) for k in range(4)]
        for box in range(boxes):
            real_sum = None
            for k, (phase_cos, phase_sin) in enumerate(phases):
                real, imag = [full_ref[8 * box + 2 * k + x, subs, lanes] for x in range(2)]
                terms = (phase_cos * real - phase_sin * imag, phase_cos * imag + phase_sin * real)
                if real_sum is None:
                    real_sum, imag_sum = terms
                else:
                    real_sum, imag_sum = real_sum + terms[0], imag_sum + terms[1]
            out_ref[0, 0, box, subs, lanes] = real_sum.astype(bf16)
            out_ref[1, 0, box, subs, lanes] = imag_sum.astype(bf16)
        return carry

    lax.fori_loop(0, (theta_rows // 16) * tiles, combine, 0)


def aggregate(held, first, halos, inner, outer, phi_matrix, phase_cos, phase_sin, flags=None):
    _, rows, _, polar, azimuths = held[0][0].shape
    theta_rows, fine = inner.shape[0], phi_matrix.shape[1]
    group = outer.shape[0]
    widths = [cols for _, cols in held]
    total = sum(widths)
    index = first // total
    masked = flags is not None
    return pl.pallas_call(
        functools.partial(aggregate_kernel, masked, group, widths),
        grid=(rows // 2, 1),
        in_specs=[pl.BlockSpec(memory_space=pltpu.SMEM)] * masked
        + [pl.BlockSpec((2, 2, cols, polar, azimuths), lambda i, j: (0, i, 0, 0, 0)) for cols in widths]
        + [
            pl.BlockSpec((2, 2, 4 * total, azimuths), lambda i, j: (0, i, index, 0)),
            pl.BlockSpec((theta_rows, polar), lambda i, j: (0, 0)),
            pl.BlockSpec((group, theta_rows, 4 * group), lambda i, j: (0, 0, 0)),
            pl.BlockSpec((azimuths, fine), lambda i, j: (0, 0)),
            pl.BlockSpec((4, theta_rows, fine), lambda i, j: (0, 0, 0)),
            pl.BlockSpec((4, theta_rows, fine), lambda i, j: (0, 0, 0)),
        ],
        out_specs=pl.BlockSpec((2, 1, total // 2, theta_rows, fine), lambda i, j: (0, i, 0, 0, 0)),
        out_shape=jax.ShapeDtypeStruct((2, rows // 2, total // 2, theta_rows, fine), jnp.bfloat16),
        scratch_shapes=[
            pltpu.VMEM((4 * total * theta_rows, azimuths), jnp.bfloat16),
            pltpu.VMEM((4 * total, theta_rows, fine), jnp.float32),
        ],
        compiler_params=pltpu.CompilerParams(vmem_limit_bytes=VMEM_BYTES),
        cost_estimate=cost(0.5 * rows * total / 4 + 1),
    )(*[flags] * masked, *[value for value, _ in held], halos, inner, outer, phi_matrix, phase_cos, phase_sin)


def runs_of(row, rows, own, sides):
    steps = [
        step
        for step in steps_of(row % 2)
        if (own if 0 <= row + step < rows else sides)
    ]
    runs = []
    for step in steps:
        kind = (abs(step) >= 2, step > 0 and abs(step) >= 2)
        if runs and runs[-1][0] == kind and runs[-1][2] == step:
            runs[-1][2] = step + 1
        else:
            runs.append([kind, step, step + 1])
    return [(kind[0], start, stop) for kind, start, stop in runs]


def translate_kernel(plan, odd_ref, dest_ref, *refs):
    own_pieces, swap_pieces, far_pieces, first, last, columns, rows, partial, final, whole = plan
    refs = list(refs)
    own_refs = [refs.pop(0) for _ in own_pieces]
    swap_refs = [refs.pop(0) for _ in swap_pieces]
    far_refs = [refs.pop(0) for _ in far_pieces]
    table_ref = refs.pop(0)
    partial_ref = refs.pop(0) if partial else None
    if whole:
        refs.pop(0)
    out_ref = refs.pop(0)
    source_ref, factor_ref = refs.pop(0), refs.pop(0)
    sum_ref = refs.pop(0) if final else None
    polar, azimuths = table_ref.shape[2], table_ref.shape[3]
    half = min(8, polar)
    even = odd_ref[0] == 0
    wide = last - first
    span = wide + 4
    f32 = jnp.float32
    at_once = 8 if wide % 8 == 0 else wide

    zero = jnp.zeros((polar, LANES), f32)

    def clear(row, carry):
        for col in range(span):
            if not 0 <= first - 2 + col < columns:
                for form in range(3):
                    source_ref[form, row, col] = zero
        return carry

    lax.fori_loop(0, rows + 4, clear, 0)

    def keep(row, col, real, imag, flag=None):
        real, imag = real.astype(f32), imag.astype(f32)
        if flag is not None:
            real, imag = real * flag, imag * flag
        source_ref[0, row, col] = real
        source_ref[1, row, col] = imag
        source_ref[2, row, col] = real + imag

    def tile(index, carry):
        lanes = pl.ds(pl.multiple_of(index * LANES, LANES), LANES)

        def keep_own(row, carry):
            for piece, (start, stop, raw) in enumerate(own_pieces):
                for col in range(max(start, first - 2), min(stop, last + 2)):
                    flag = dest_ref[row, col].astype(f32) if raw else None
                    keep(row + 2, col - (first - 2), *[own_refs[piece][x, row, col - start, :, lanes] for x in range(2)], flag)
            return carry

        def keep_sides(row, carry):
            def load(pieces, piece_refs, col):
                ref, at = [
                    (ref, col - start) for ref, (start, stop) in zip(piece_refs, pieces) if start <= col < stop
                ][0]
                return [ref[x, row, at, :, lanes] for x in range(2)]

            for col in range(max(0, first - 2), min(columns, last + 2)):
                swap, far = load(swap_pieces, swap_refs, col), load(far_pieces, far_refs, col)
                to = col - (first - 2)
                keep(row, to, *[jnp.where(even, far[x], swap[x]) for x in range(2)])
                keep(rows + 2 + row, to, *[jnp.where(even, swap[x], far[x]) for x in range(2)])
            return carry

        if own_pieces:
            lax.fori_loop(0, rows, keep_own, 0)
        if swap_pieces:
            lax.fori_loop(0, 2, keep_sides, 0)

        def keep_factors(block, carry):
            for code in [block * 4 + n for n in range(4)]:
                real = table_ref[0, code, :, lanes].astype(f32)
                imag = table_ref[1, code, :, lanes].astype(f32)
                factor_ref[0, code] = real
                factor_ref[1, code] = imag - real
                factor_ref[2, code] = imag + real
            return carry

        lax.fori_loop(0, len(far_offsets) // 4, keep_factors, 0)

        def part(index, carry):
            subs = pl.ds(pl.multiple_of((index % (polar // half)) * half, half), half)
            begin = (index // (polar // half)) * at_once
            for row in range(rows):

                def one_step(far_row, base, start, row=row):
                    cols = [q for q in range(-3, 4) if far_row or abs(q) >= 2]

                    def body(step, sums):
                        sums = [list(s) for s in sums]
                        found = {}
                        code = base + step * len(cols)
                        for n, step_col in enumerate(cols):
                            factor = [factor_ref[form, code + n, subs] for form in range(3)]
                            for dest in range(at_once):
                                if step_col not in steps_of(dest % 2):
                                    continue
                                col = dest + 2 + step_col
                                if col not in found:
                                    found[col] = [
                                        source_ref[form, row + 2 + start + step, begin + col, subs]
                                        for form in range(3)
                                    ]
                                real, imag, both = found[col]
                                terms = (both * factor[0], real * factor[1], imag * factor[2])
                                sums[dest] = [s + t for s, t in zip(sums[dest], terms)]
                        return tuple(tuple(s) for s in sums)

                    return body

                nothing = jnp.zeros((half, LANES), f32)
                sums = tuple((nothing,) * 3 for _ in range(at_once))
                for far_row, start, stop in runs_of(row, rows, bool(own_pieces), bool(swap_pieces)):
                    base = code_of[start, -3]
                    sums = lax.fori_loop(0, stop - start, one_step(far_row, base, start), sums)
                for dest in range(at_once):
                    shared, cross, other = sums[dest]
                    pair = [shared - other, shared + cross]
                    for x in range(2):
                        value = pair[x]
                        if partial:
                            value = value + partial_ref[x, row, begin + dest, subs, lanes]
                        if final:
                            flag = dest_ref[row, first + begin + dest].astype(f32)
                            sum_ref[x, row, begin + dest, subs] = value * flag
                        else:
                            out_ref[x, row, begin + dest, subs, lanes] = value
            return carry

        lax.fori_loop(0, (polar // half) * (wide // at_once), part, 0)

        def finish(row, carry):
            for x in range(2):
                for dest in range(wide):
                    out_ref[x, row, dest, :, lanes] = sum_ref[x, row, dest].astype(jnp.bfloat16)
            return carry

        if final:
            lax.fori_loop(0, rows, finish, 0)
        return carry

    lax.fori_loop(0, azimuths // LANES, tile, 0)


def translate(own, sides, table, dest, odd, first, last, partial=None, final=True, whole=None, raw=False, part=(0, 1)):
    rows, columns = dest.shape
    polar, azimuths = table.shape[2], table.shape[3]
    block = min(16, polar)
    edge = rows // 2 - 1
    wide = last - first
    steps = polar // block // part[1]
    skip = part[0] * steps

    own_pieces = [(0, columns, raw)] if own else []
    swap_side, far_side = [
        [chunk for chunk in side if chunk[1] < last + 2 and chunk[2] > first - 2] for side in sides or ([], [])
    ]
    at = first // wide
    operands = list(own)
    specs = [
        pl.BlockSpec((2, rows, stop - start, block, azimuths), lambda t, odd, dest: (0, 0, 0, t + skip, 0))
        for start, stop, _ in own_pieces
    ]
    for side, place in ((swap_side, lambda odd: odd), (far_side, lambda odd: 1 - odd)):
        operands += [held for held, start, stop in side]
        specs += [
            pl.BlockSpec(
                (2, 2, stop - start, block, azimuths),
                lambda t, odd, dest, place=place: (0, place(odd[0]) * edge, 0, t + skip, 0),
            )
            for held, start, stop in side
        ]
    operands.append(table)
    specs.append(pl.BlockSpec((2, len(far_offsets), block, azimuths), lambda t, odd, dest: (0, 0, t + skip, 0)))
    out_spec = pl.BlockSpec((2, rows, wide, block, azimuths), lambda t, odd, dest: (0, 0, at, t + skip, 0))
    if partial is not None:
        operands.append(partial)
        specs.append(out_spec)
    aliases = {}
    if whole is not None:
        operands.append(whole)
        specs.append(pl.BlockSpec(memory_space=pl.ANY))
        aliases = {len(operands) + 1: 0}
    kind = jnp.bfloat16 if final else jnp.float32
    scratch = [
        pltpu.VMEM((3, rows + 4, wide + 4, block, LANES), jnp.float32),
        pltpu.VMEM((3, len(far_offsets), block, LANES), jnp.float32),
    ]
    if final:
        scratch.append(pltpu.VMEM((2, rows, wide, block, LANES), jnp.float32))
    swap_pieces, far_pieces = [[chunk[1:] for chunk in side] for side in (swap_side, far_side)]
    plan = (own_pieces, swap_pieces, far_pieces, first, last, columns, rows, partial is not None, final, whole is not None)
    share = ((2 / 3 if rows > 2 else 2 / 9) if own else 0) + ((1 / 3 if rows > 2 else 7 / 9) if sides else 0)
    return pl.pallas_call(
        functools.partial(translate_kernel, plan),
        grid_spec=pltpu.PrefetchScalarGridSpec(
            num_scalar_prefetch=2,
            grid=(steps,),
            in_specs=specs,
            out_specs=out_spec,
            scratch_shapes=scratch,
        ),
        out_shape=jax.ShapeDtypeStruct((2, rows, columns, polar, azimuths), kind),
        input_output_aliases=aliases,
        compiler_params=pltpu.CompilerParams(vmem_limit_bytes=VMEM_BYTES),
        cost_estimate=cost(22 * share * wide / columns / part[1] + 1),
    )(odd, dest, *operands)


def local(pattern, occupied, trans_fine, trans_coarse, theta_weights, phi_matrix, child_phase):
    _, count_rows, count_cols, polar, azimuths = pattern.shape
    groups = lax.axis_size("box")
    odd = (lax.axis_index("box") % 2).astype(jnp.int32).reshape(1)
    partner = [(i, i ^ 1) for i in range(groups)]
    onward = [(i, i + 2) for i in range(0, groups - 2, 2)] + [(i, i - 2) for i in range(3, groups, 2)]
    group = count_cols // 4
    widths = [3 * group // 2, 3 * group // 2, group]
    starts = [0, widths[0], 2 * widths[0], count_cols]

    def flat(held):
        return held.reshape(2, count_rows, -1, azimuths)

    def placed(held, cols):
        ends = [sum(cols[: k + 1]) for k in range(len(cols))]
        return [(value, end - size, end) for value, size, end in zip(held, cols, ends)]

    def send(value, pairs):
        return lax.ppermute(value, "box", pairs)

    fine_plan = (trans_fine, occupied, odd)
    occupied_coarse = jnp.max(occupied.reshape(count_rows // 2, 2, count_cols // 2, 2), axis=(1, 3))
    coarse_plan = (trans_coarse, occupied_coarse, odd)
    half = count_cols // 2

    own0 = mask_first(pattern, occupied, widths[0])
    rest, flags, own0 = lax.optimization_barrier((pattern, occupied, own0))
    flags = flags.astype(jnp.bfloat16)[None, :, :, None, None]

    def chunk(values, k):
        return values[:, :, starts[k] : starts[k + 1]] * flags[:, :, starts[k] : starts[k + 1]]

    swap0 = send(own0, partner)
    edges = jnp.concatenate([rest[:, :, :, :2], rest[:, :, :, -2:]], axis=3) * flags
    beside = halo(edges)
    fine_sums = translate([rest], None, *fine_plan, 0, count_cols, final=False, raw=True)
    own1, own2 = chunk(rest, 1), chunk(rest, 2)
    swap0, fine_sums, beside, own1, own2, rest, child_phase = lax.optimization_barrier(
        (swap0, fine_sums, beside, own1, own2, rest, child_phase)
    )

    own_halo = jnp.concatenate(beside, axis=3).reshape(2, count_rows, -1, polar, azimuths)
    swap1 = send(jnp.concatenate([own1, own_halo], axis=2), partner)
    far0 = send(swap0, onward)
    phases = (jnp.cos(child_phase), jnp.sin(child_phase))
    fixed = (*bands(theta_weights, polar, group), phi_matrix, *phases)
    coarse_own = aggregate([(rest, count_cols)], 0, flat(own_halo), *fixed, flags=occupied)
    swap0, swap1, far0, coarse_own, own2 = lax.optimization_barrier((swap0, swap1, far0, coarse_own, own2))

    swap2 = send(own2, partner)
    far1 = send(swap1, onward)
    swap_halo = flat(swap1[:, :, widths[1] :])
    coarse_swap = [aggregate([(swap0, widths[0]), (swap1, widths[1])], 0, swap_halo, *fixed)]
    coarse_sums = translate([coarse_own], None, *coarse_plan, 0, half, final=False)
    swap2, far1, coarse_swap, swap_halo, coarse_sums = lax.optimization_barrier(
        (swap2, far1, coarse_swap, swap_halo, coarse_sums)
    )

    far2 = send(swap2, onward)
    far_halo = flat(far1[:, :, widths[1] :])
    coarse_far = [aggregate([(far0, widths[0]), (far1, widths[1])], 0, far_halo, *fixed)]
    coarse_swap.append(aggregate([(swap2, widths[2])], starts[2], swap_halo, *fixed))
    far2, coarse_far, coarse_swap = lax.optimization_barrier((far2, coarse_far, coarse_swap))

    coarse_far.append(aggregate([(far2, widths[2])], starts[2], far_halo, *fixed))
    coarse_sides = [placed(held, [3 * group // 2, group // 2]) for held in (coarse_swap, coarse_far)]
    local_coarse = translate([], coarse_sides, *coarse_plan, 0, half, partial=coarse_sums)
    fine_sides = [placed(held, widths) for held in ((swap0, swap1, swap2), (far0, far1, far2))]
    local_fine = translate([], fine_sides, *fine_plan, 0, count_cols, partial=fine_sums)
    return local_fine, local_coarse


def solution(mesh):
    return jax.shard_map(
        local,
        mesh=mesh,
        in_specs=(
            P(None, "box", None, "dir", None),
            P("box", None),
            P(None, None, "dir", None),
            P(None, None, "dir", None),
            P("dir", None),
            P(),
            P(None, "dir", None),
        ),
        out_specs=(P(None, "box", None, "dir", None), P(None, "box", None, "dir", None)),
        check_vma=False,
    )
```

```python
import functools

import jax
import jax.numpy as jnp
from jax import lax
from jax.experimental import pallas as pl
from jax.experimental.pallas import tpu as pltpu
from jax.sharding import PartitionSpec as P

far_offsets = [
    (step_row, step_col)
    for step_row in range(-3, 4)
    for step_col in range(-3, 4)
    if max(abs(step_row), abs(step_col)) >= 2
]
code_of = {step: code for code, step in enumerate(far_offsets)}
LANES = 128
VMEM_BYTES = 48 * 2**20


def steps_of(parity):
    return range(-3, 3) if parity else range(-2, 4)


def halo(masked):
    size = lax.axis_size("dir")
    up = [(i, i + 1) for i in range(size - 1)]
    down = [(j, i) for i, j in up]
    before = lax.ppermute(masked[:, :, :, -2:], "dir", up)
    after = lax.ppermute(masked[:, :, :, :2], "dir", down)
    return before, after


def bands(theta_weights, rows, group):
    theta_rows = theta_weights.shape[0]
    row_ids = jnp.arange(theta_rows, dtype=jnp.int32)[:, None]
    col_ids = jnp.arange(rows + 4, dtype=jnp.int32)[None, :]
    band = jnp.zeros((theta_rows, rows + 4), jnp.float32)
    for stencil in range(4):
        band = band + jnp.where(
            col_ids == row_ids // 2 + 1 + stencil,
            theta_weights[:, stencil : stencil + 1].astype(jnp.float32),
            0.0,
        )
    band = band.astype(jnp.bfloat16)
    inner = band[:, 2 : rows + 2]
    outer = jnp.concatenate([band[:, :2], band[:, rows + 2 :]], axis=1)
    outer = jnp.stack(
        [jnp.pad(outer, ((0, 0), (4 * c, 4 * (group - 1 - c)))) for c in range(group)]
    )
    return inner, outer


def cost(us):
    return pl.CostEstimate(flops=0, bytes_accessed=int(us * 3.3e5), transcendentals=0)


def mask_kernel(flag_ref, pattern_ref, out_ref):
    for row in range(out_ref.shape[1]):
        for col in range(out_ref.shape[2]):
            flag = flag_ref[row, col].astype(jnp.float32).astype(jnp.bfloat16)
            for x in range(2):
                out_ref[x, row, col] = pattern_ref[x, row, col] * flag


def mask_first(pattern, occupied, width):
    _, rows, _, polar, azimuths = pattern.shape
    shape = (2, rows, width, polar, azimuths)
    spec = pl.BlockSpec(shape, lambda i: (0, 0, 0, 0, 0))
    return pl.pallas_call(
        mask_kernel,
        grid=(1,),
        in_specs=[pl.BlockSpec(memory_space=pltpu.SMEM), spec],
        out_specs=spec,
        out_shape=jax.ShapeDtypeStruct(shape, jnp.bfloat16),
        compiler_params=pltpu.CompilerParams(vmem_limit_bytes=60 * 2**20),
        cost_estimate=cost(1),
    )(occupied, pattern)


def aggregate_kernel(masked, group, first, widths, *refs):
    refs = list(refs)
    flag_ref = refs.pop(0) if masked else None
    m_refs = [refs.pop(0) for _ in widths]
    columns = [(ref, at) for ref, width in zip(m_refs, widths) for at in range(width)]
    h_ref, inner_ref, outer_ref, phi_ref, cos_ref, sin_ref, out_ref, part_ref, full_ref = refs
    theta_rows, polar = inner_ref.shape
    boxes = out_ref.shape[2]
    azimuths, fine = phi_ref.shape
    f32, bf16 = jnp.float32, jnp.bfloat16
    pairs = [(x, a) for x in range(2) for a in range(2)]
    for col in range(2 * boxes):
        ref, column = columns[col]
        blocks = [ref[x, a, column] for x, a in pairs]
        if masked:
            row, at = 2 * pl.program_id(0), 2 * boxes * pl.program_id(1) + col
            flags = [flag_ref[row + a, at].astype(f32).astype(bf16) for x, a in pairs]
            blocks = [block * flag for block, flag in zip(blocks, flags)]
        own = jnp.concatenate(blocks, axis=1)
        rows = pl.ds((first + col) // group * 4 * group, 4 * group)
        beside = jnp.concatenate([h_ref[x, a, rows] for x, a in pairs], axis=1)
        outer = outer_ref[(first + col) % group]
        if polar % 16 == 0:
            both = jnp.concatenate([inner_ref[...], outer], axis=1)
            part = jnp.dot(both, jnp.concatenate([own, beside], axis=0), preferred_element_type=f32)
        else:
            part = jnp.dot(inner_ref[...], own, preferred_element_type=f32)
            part = part + jnp.dot(outer, beside, preferred_element_type=f32)
        part = part.astype(bf16)
        for n, (x, a) in enumerate(pairs):
            slot = ((col // 2) * 4 + 2 * a + col % 2) * 2 + x
            part_ref[pl.ds(slot * theta_rows, theta_rows), :] = part[:, n * azimuths : (n + 1) * azimuths]
    full = jnp.dot(part_ref[...], phi_ref[...], preferred_element_type=f32)
    full_ref[...] = full.reshape(full_ref.shape)
    tiles = fine // LANES

    def combine(index, carry):
        start = pl.multiple_of((index // tiles) * 16, 16)
        subs = pl.ds(start, 16)
        lanes = pl.ds(pl.multiple_of((index % tiles) * LANES, LANES), LANES)
        phases = [(cos_ref[k, subs, lanes], sin_ref[k, subs, lanes]) for k in range(4)]
        for box in range(boxes):
            real_sum = None
            for k, (phase_cos, phase_sin) in enumerate(phases):
                real, imag = [full_ref[8 * box + 2 * k + x, subs, lanes] for x in range(2)]
                terms = (phase_cos * real - phase_sin * imag, phase_cos * imag + phase_sin * real)
                if real_sum is None:
                    real_sum, imag_sum = terms
                else:
                    real_sum, imag_sum = real_sum + terms[0], imag_sum + terms[1]
            out_ref[0, 0, box, subs, lanes] = real_sum.astype(bf16)
            out_ref[1, 0, box, subs, lanes] = imag_sum.astype(bf16)
        return carry

    lax.fori_loop(0, (theta_rows // 16) * tiles, combine, 0)


def aggregate(held, first, halos, inner, outer, phi_matrix, phase_cos, phase_sin, flags=None):
    _, rows, _, polar, azimuths = held[0][0].shape
    theta_rows, fine = inner.shape[0], phi_matrix.shape[1]
    group = outer.shape[0]
    widths = [cols for _, cols in held]
    total = sum(widths)
    beside = halos.shape[2]
    masked = flags is not None
    return pl.pallas_call(
        functools.partial(aggregate_kernel, masked, group, first, widths),
        grid=(rows // 2, 1),
        in_specs=[pl.BlockSpec(memory_space=pltpu.SMEM)] * masked
        + [pl.BlockSpec((2, 2, cols, polar, azimuths), lambda i, j: (0, i, 0, 0, 0)) for cols in widths]
        + [
            pl.BlockSpec((2, 2, beside, azimuths), lambda i, j: (0, i, 0, 0)),
            pl.BlockSpec((theta_rows, polar), lambda i, j: (0, 0)),
            pl.BlockSpec((group, theta_rows, 4 * group), lambda i, j: (0, 0, 0)),
            pl.BlockSpec((azimuths, fine), lambda i, j: (0, 0)),
            pl.BlockSpec((4, theta_rows, fine), lambda i, j: (0, 0, 0)),
            pl.BlockSpec((4, theta_rows, fine), lambda i, j: (0, 0, 0)),
        ],
        out_specs=pl.BlockSpec((2, 1, total // 2, theta_rows, fine), lambda i, j: (0, i, 0, 0, 0)),
        out_shape=jax.ShapeDtypeStruct((2, rows // 2, total // 2, theta_rows, fine), jnp.bfloat16),
        scratch_shapes=[
            pltpu.VMEM((4 * total * theta_rows, azimuths), jnp.bfloat16),
            pltpu.VMEM((4 * total, theta_rows, fine), jnp.float32),
        ],
        compiler_params=pltpu.CompilerParams(vmem_limit_bytes=VMEM_BYTES),
        cost_estimate=cost(0.5 * rows * total / 4 + 1),
    )(*[flags] * masked, *[value for value, _ in held], halos, inner, outer, phi_matrix, phase_cos, phase_sin)


def runs_of(row, rows, own, sides):
    steps = [
        step
        for step in steps_of(row % 2)
        if (own if 0 <= row + step < rows else sides)
    ]
    runs = []
    for step in steps:
        kind = (abs(step) >= 2, step > 0 and abs(step) >= 2)
        if runs and runs[-1][0] == kind and runs[-1][2] == step:
            runs[-1][2] = step + 1
        else:
            runs.append([kind, step, step + 1])
    return [(kind[0], start, stop) for kind, start, stop in runs]


def translate_kernel(plan, odd_ref, dest_ref, *refs):
    own_pieces, swap_pieces, far_pieces, first, last, columns, rows, partial, final, whole = plan
    refs = list(refs)
    own_refs = [refs.pop(0) for _ in own_pieces]
    swap_refs = [refs.pop(0) for _ in swap_pieces]
    far_refs = [refs.pop(0) for _ in far_pieces]
    table_ref = refs.pop(0)
    partial_ref = refs.pop(0) if partial else None
    if whole:
        refs.pop(0)
    out_ref = refs.pop(0)
    source_ref, factor_ref = refs.pop(0), refs.pop(0)
    sum_ref = refs.pop(0) if final else None
    polar, azimuths = table_ref.shape[2], table_ref.shape[3]
    half = min(8, polar)
    even = odd_ref[0] == 0
    wide = last - first
    span = wide + 4
    f32 = jnp.float32
    at_once = 8 if wide % 8 == 0 else wide

    zero = jnp.zeros((polar, LANES), f32)

    def clear(row, carry):
        for col in range(span):
            if not 0 <= first - 2 + col < columns:
                for form in range(3):
                    source_ref[form, row, col] = zero
        return carry

    lax.fori_loop(0, rows + 4, clear, 0)

    def keep(row, col, real, imag, flag=None):
        real, imag = real.astype(f32), imag.astype(f32)
        if flag is not None:
            real, imag = real * flag, imag * flag
        source_ref[0, row, col] = real
        source_ref[1, row, col] = imag
        source_ref[2, row, col] = real + imag

    def tile(index, carry):
        lanes = pl.ds(pl.multiple_of(index * LANES, LANES), LANES)

        def keep_own(row, carry):
            for piece, (start, stop, raw) in enumerate(own_pieces):
                for col in range(max(start, first - 2), min(stop, last + 2)):
                    flag = dest_ref[row, col].astype(f32) if raw else None
                    keep(row + 2, col - (first - 2), *[own_refs[piece][x, row, col - start, :, lanes] for x in range(2)], flag)
            return carry

        def keep_sides(row, carry):
            def load(pieces, piece_refs, col):
                ref, at = [
                    (ref, col - start) for ref, (start, stop) in zip(piece_refs, pieces) if start <= col < stop
                ][0]
                return [ref[x, row, at, :, lanes] for x in range(2)]

            for col in range(max(0, first - 2), min(columns, last + 2)):
                swap, far = load(swap_pieces, swap_refs, col), load(far_pieces, far_refs, col)
                to = col - (first - 2)
                keep(row, to, *[jnp.where(even, far[x], swap[x]) for x in range(2)])
                keep(rows + 2 + row, to, *[jnp.where(even, swap[x], far[x]) for x in range(2)])
            return carry

        if own_pieces:
            lax.fori_loop(0, rows, keep_own, 0)
        if swap_pieces:
            lax.fori_loop(0, 2, keep_sides, 0)

        def keep_factors(block, carry):
            for code in [block * 4 + n for n in range(4)]:
                real = table_ref[0, code, :, lanes].astype(f32)
                imag = table_ref[1, code, :, lanes].astype(f32)
                factor_ref[0, code] = real
                factor_ref[1, code] = imag - real
                factor_ref[2, code] = imag + real
            return carry

        lax.fori_loop(0, len(far_offsets) // 4, keep_factors, 0)

        def part(index, carry):
            subs = pl.ds(pl.multiple_of((index % (polar // half)) * half, half), half)
            begin = (index // (polar // half)) * at_once
            for row in range(rows):

                def one_step(far_row, base, start, row=row):
                    cols = [q for q in range(-3, 4) if far_row or abs(q) >= 2]

                    def body(step, sums):
                        sums = [list(s) for s in sums]
                        found = {}
                        code = base + step * len(cols)
                        for n, step_col in enumerate(cols):
                            factor = [factor_ref[form, code + n, subs] for form in range(3)]
                            for dest in range(at_once):
                                if step_col not in steps_of(dest % 2):
                                    continue
                                col = dest + 2 + step_col
                                if col not in found:
                                    found[col] = [
                                        source_ref[form, row + 2 + start + step, begin + col, subs]
                                        for form in range(3)
                                    ]
                                real, imag, both = found[col]
                                terms = (both * factor[0], real * factor[1], imag * factor[2])
                                sums[dest] = [s + t for s, t in zip(sums[dest], terms)]
                        return tuple(tuple(s) for s in sums)

                    return body

                nothing = jnp.zeros((half, LANES), f32)
                sums = tuple((nothing,) * 3 for _ in range(at_once))
                for far_row, start, stop in runs_of(row, rows, bool(own_pieces), bool(swap_pieces)):
                    base = code_of[start, -3]
                    sums = lax.fori_loop(0, stop - start, one_step(far_row, base, start), sums)
                for dest in range(at_once):
                    shared, cross, other = sums[dest]
                    pair = [shared - other, shared + cross]
                    for x in range(2):
                        value = pair[x]
                        if partial:
                            value = value + partial_ref[x, row, begin + dest, subs, lanes]
                        if final:
                            flag = dest_ref[row, first + begin + dest].astype(f32)
                            sum_ref[x, row, begin + dest, subs] = value * flag
                        else:
                            out_ref[x, row, begin + dest, subs, lanes] = value
            return carry

        lax.fori_loop(0, (polar // half) * (wide // at_once), part, 0)

        def finish(row, carry):
            for x in range(2):
                for dest in range(wide):
                    out_ref[x, row, dest, :, lanes] = sum_ref[x, row, dest].astype(jnp.bfloat16)
            return carry

        if final:
            lax.fori_loop(0, rows, finish, 0)
        return carry

    lax.fori_loop(0, azimuths // LANES, tile, 0)


def translate(own, sides, table, dest, odd, first, last, partial=None, final=True, whole=None, raw=False, part=(0, 1)):
    rows, columns = dest.shape
    polar, azimuths = table.shape[2], table.shape[3]
    block = min(16, polar)
    edge = rows // 2 - 1
    wide = last - first
    steps = polar // block // part[1]
    skip = part[0] * steps

    own_pieces = [(0, columns, raw)] if own else []
    swap_side, far_side = [
        [chunk for chunk in side if chunk[1] < last + 2 and chunk[2] > first - 2] for side in sides or ([], [])
    ]
    at = first // wide
    operands = list(own)
    specs = [
        pl.BlockSpec((2, rows, stop - start, block, azimuths), lambda t, odd, dest: (0, 0, 0, t + skip, 0))
        for start, stop, _ in own_pieces
    ]
    for side, place in ((swap_side, lambda odd: odd), (far_side, lambda odd: 1 - odd)):
        operands += [held for held, start, stop in side]
        specs += [
            pl.BlockSpec(
                (2, 2, stop - start, block, azimuths),
                lambda t, odd, dest, place=place: (0, place(odd[0]) * edge, 0, t + skip, 0),
            )
            for held, start, stop in side
        ]
    operands.append(table)
    specs.append(pl.BlockSpec((2, len(far_offsets), block, azimuths), lambda t, odd, dest: (0, 0, t + skip, 0)))
    out_spec = pl.BlockSpec((2, rows, wide, block, azimuths), lambda t, odd, dest: (0, 0, at, t + skip, 0))
    if partial is not None:
        operands.append(partial)
        specs.append(out_spec)
    aliases = {}
    if whole is not None:
        operands.append(whole)
        specs.append(pl.BlockSpec(memory_space=pl.ANY))
        aliases = {len(operands) + 1: 0}
    kind = jnp.bfloat16 if final else jnp.float32
    scratch = [
        pltpu.VMEM((3, rows + 4, wide + 4, block, LANES), jnp.float32),
        pltpu.VMEM((3, len(far_offsets), block, LANES), jnp.float32),
    ]
    if final:
        scratch.append(pltpu.VMEM((2, rows, wide, block, LANES), jnp.float32))
    swap_pieces, far_pieces = [[chunk[1:] for chunk in side] for side in (swap_side, far_side)]
    plan = (own_pieces, swap_pieces, far_pieces, first, last, columns, rows, partial is not None, final, whole is not None)
    share = ((2 / 3 if rows > 2 else 2 / 9) if own else 0) + ((1 / 3 if rows > 2 else 7 / 9) if sides else 0)
    return pl.pallas_call(
        functools.partial(translate_kernel, plan),
        grid_spec=pltpu.PrefetchScalarGridSpec(
            num_scalar_prefetch=2,
            grid=(steps,),
            in_specs=specs,
            out_specs=out_spec,
            scratch_shapes=scratch,
        ),
        out_shape=jax.ShapeDtypeStruct((2, rows, columns, polar, azimuths), kind),
        input_output_aliases=aliases,
        compiler_params=pltpu.CompilerParams(vmem_limit_bytes=VMEM_BYTES),
        cost_estimate=cost(22 * share * wide / columns / part[1] + 1),
    )(odd, dest, *operands)


def local(pattern, occupied, trans_fine, trans_coarse, theta_weights, phi_matrix, child_phase):
    _, count_rows, count_cols, polar, azimuths = pattern.shape
    groups = lax.axis_size("box")
    odd = (lax.axis_index("box") % 2).astype(jnp.int32).reshape(1)
    partner = [(i, i ^ 1) for i in range(groups)]
    onward = [(i, i + 2) for i in range(0, groups - 2, 2)] + [(i, i - 2) for i in range(3, groups, 2)]
    group = count_cols // 4
    widths = [3 * group // 2, group, 3 * group // 2]
    starts = [0, widths[0], widths[0] + group, count_cols]

    def flat(held):
        return held.reshape(2, count_rows, -1, azimuths)

    def placed(held, cols):
        ends = [sum(cols[: k + 1]) for k in range(len(cols))]
        return [(value, end - size, end) for value, size, end in zip(held, cols, ends)]

    def send(value, pairs):
        return lax.ppermute(value, "box", pairs)

    fine_plan = (trans_fine, occupied, odd)
    occupied_coarse = jnp.max(occupied.reshape(count_rows // 2, 2, count_cols // 2, 2), axis=(1, 3))
    coarse_plan = (trans_coarse, occupied_coarse, odd)
    half = count_cols // 2

    own0 = mask_first(pattern, occupied, widths[0])
    rest, flags, own0 = lax.optimization_barrier((pattern, occupied, own0))
    flags = flags.astype(jnp.bfloat16)[None, :, :, None, None]

    def chunk(values, k):
        return values[:, :, starts[k] : starts[k + 1]] * flags[:, :, starts[k] : starts[k + 1]]

    swap0 = send(own0, partner)
    edges = jnp.concatenate([rest[:, :, :, :2], rest[:, :, :, -2:]], axis=3) * flags
    beside = halo(edges)
    fine_sums = translate([rest], None, *fine_plan, 0, count_cols, final=False, raw=True)
    own1, own2 = chunk(rest, 1), chunk(rest, 2)
    swap0, fine_sums, beside, own1, own2, rest, child_phase = lax.optimization_barrier(
        (swap0, fine_sums, beside, own1, own2, rest, child_phase)
    )

    own_halo = jnp.concatenate(beside, axis=3).reshape(2, count_rows, -1, polar, azimuths)
    swap1 = send(jnp.concatenate([own1, own_halo], axis=2), partner)
    far0 = send(swap0, onward)
    phases = (jnp.cos(child_phase), jnp.sin(child_phase))
    fixed = (*bands(theta_weights, polar, group), phi_matrix, *phases)
    coarse_own = aggregate([(rest, count_cols)], 0, flat(own_halo), *fixed, flags=occupied)
    swap0, swap1, far0, coarse_own, own2 = lax.optimization_barrier((swap0, swap1, far0, coarse_own, own2))

    swap2 = send(own2, partner)
    far1 = send(swap1, onward)
    swap_halo = flat(swap1[:, :, widths[1] :])
    coarse_swap = [aggregate([(swap0, widths[0]), (swap1, widths[1])], 0, swap_halo, *fixed)]
    coarse_sums = translate([coarse_own], None, *coarse_plan, 0, half, final=False)
    swap2, far1, coarse_swap, swap_halo, coarse_sums = lax.optimization_barrier(
        (swap2, far1, coarse_swap, swap_halo, coarse_sums)
    )

    far2 = send(swap2, onward)
    far_halo = flat(far1[:, :, widths[1] :])
    coarse_far = [aggregate([(far0, widths[0]), (far1, widths[1])], 0, far_halo, *fixed)]
    coarse_swap.append(aggregate([(swap2, widths[2])], starts[2], swap_halo, *fixed))
    far2, coarse_far, coarse_swap = lax.optimization_barrier((far2, coarse_far, coarse_swap))

    coarse_far.append(aggregate([(far2, widths[2])], starts[2], far_halo, *fixed))
    coarse_sides = [placed(held, [starts[2] // 2, widths[2] // 2]) for held in (coarse_swap, coarse_far)]
    local_coarse = translate([], coarse_sides, *coarse_plan, 0, half, partial=coarse_sums)
    fine_sides = [placed(held, widths) for held in ((swap0, swap1, swap2), (far0, far1, far2))]
    local_fine = translate([], fine_sides, *fine_plan, 0, count_cols, partial=fine_sums)
    return local_fine, local_coarse


def solution(mesh):
    return jax.shard_map(
        local,
        mesh=mesh,
        in_specs=(
            P(None, "box", None, "dir", None),
            P("box", None),
            P(None, None, "dir", None),
            P(None, None, "dir", None),
            P("dir", None),
            P(),
            P(None, "dir", None),
        ),
        out_specs=(P(None, "box", None, "dir", None), P(None, "box", None, "dir", None)),
        check_vma=False,
    )
```

```python
import functools

import jax
import jax.numpy as jnp
from jax import lax
from jax.experimental import pallas as pl
from jax.experimental.pallas import tpu as pltpu
from jax.sharding import PartitionSpec as P

far_offsets = [
    (step_row, step_col)
    for step_row in range(-3, 4)
    for step_col in range(-3, 4)
    if max(abs(step_row), abs(step_col)) >= 2
]
code_of = {step: code for code, step in enumerate(far_offsets)}
LANES = 128
VMEM_BYTES = 48 * 2**20


def steps_of(parity):
    return range(-3, 3) if parity else range(-2, 4)


def halo(masked):
    size = lax.axis_size("dir")
    up = [(i, i + 1) for i in range(size - 1)]
    down = [(j, i) for i, j in up]
    before = lax.ppermute(masked[:, :, :, -2:], "dir", up)
    after = lax.ppermute(masked[:, :, :, :2], "dir", down)
    return before, after


def bands(theta_weights, rows, group):
    theta_rows = theta_weights.shape[0]
    row_ids = jnp.arange(theta_rows, dtype=jnp.int32)[:, None]
    col_ids = jnp.arange(rows + 4, dtype=jnp.int32)[None, :]
    band = jnp.zeros((theta_rows, rows + 4), jnp.float32)
    for stencil in range(4):
        band = band + jnp.where(
            col_ids == row_ids // 2 + 1 + stencil,
            theta_weights[:, stencil : stencil + 1].astype(jnp.float32),
            0.0,
        )
    band = band.astype(jnp.bfloat16)
    inner = band[:, 2 : rows + 2]
    outer = jnp.concatenate([band[:, :2], band[:, rows + 2 :]], axis=1)
    outer = jnp.stack(
        [jnp.pad(outer, ((0, 0), (4 * c, 4 * (group - 1 - c)))) for c in range(group)]
    )
    return inner, outer


def cost(us):
    return pl.CostEstimate(flops=0, bytes_accessed=int(us * 3.3e5), transcendentals=0)


def mask_kernel(flag_ref, pattern_ref, out_ref):
    for row in range(out_ref.shape[1]):
        for col in range(out_ref.shape[2]):
            flag = flag_ref[row, col].astype(jnp.float32).astype(jnp.bfloat16)
            for x in range(2):
                out_ref[x, row, col] = pattern_ref[x, row, col] * flag


def mask_first(pattern, occupied, width):
    _, rows, _, polar, azimuths = pattern.shape
    shape = (2, rows, width, polar, azimuths)
    spec = pl.BlockSpec(shape, lambda i: (0, 0, 0, 0, 0))
    return pl.pallas_call(
        mask_kernel,
        grid=(1,),
        in_specs=[pl.BlockSpec(memory_space=pltpu.SMEM), spec],
        out_specs=spec,
        out_shape=jax.ShapeDtypeStruct(shape, jnp.bfloat16),
        compiler_params=pltpu.CompilerParams(vmem_limit_bytes=60 * 2**20),
        cost_estimate=cost(1),
    )(occupied, pattern)


def aggregate_kernel(masked, group, first, widths, *refs):
    refs = list(refs)
    flag_ref = refs.pop(0) if masked else None
    m_refs = [refs.pop(0) for _ in widths]
    columns = [(ref, at) for ref, width in zip(m_refs, widths) for at in range(width)]
    h_ref, inner_ref, outer_ref, phi_ref, cos_ref, sin_ref, out_ref, part_ref, full_ref = refs
    theta_rows, polar = inner_ref.shape
    boxes = out_ref.shape[2]
    azimuths, fine = phi_ref.shape
    f32, bf16 = jnp.float32, jnp.bfloat16
    pairs = [(x, a) for x in range(2) for a in range(2)]
    for col in range(2 * boxes):
        ref, column = columns[col]
        blocks = [ref[x, a, column] for x, a in pairs]
        if masked:
            row, at = 2 * pl.program_id(0), 2 * boxes * pl.program_id(1) + col
            flags = [flag_ref[row + a, at].astype(f32).astype(bf16) for x, a in pairs]
            blocks = [block * flag for block, flag in zip(blocks, flags)]
        own = jnp.concatenate(blocks, axis=1)
        rows = pl.ds((first + col) // group * 4 * group, 4 * group)
        beside = jnp.concatenate([h_ref[x, a, rows] for x, a in pairs], axis=1)
        outer = outer_ref[(first + col) % group]
        if polar % 16 == 0:
            both = jnp.concatenate([inner_ref[...], outer], axis=1)
            part = jnp.dot(both, jnp.concatenate([own, beside], axis=0), preferred_element_type=f32)
        else:
            part = jnp.dot(inner_ref[...], own, preferred_element_type=f32)
            part = part + jnp.dot(outer, beside, preferred_element_type=f32)
        part = part.astype(bf16)
        for n, (x, a) in enumerate(pairs):
            slot = ((col // 2) * 4 + 2 * a + col % 2) * 2 + x
            part_ref[pl.ds(slot * theta_rows, theta_rows), :] = part[:, n * azimuths : (n + 1) * azimuths]
    full = jnp.dot(part_ref[...], phi_ref[...], preferred_element_type=f32)
    full_ref[...] = full.reshape(full_ref.shape)
    tiles = fine // LANES

    def combine(index, carry):
        start = pl.multiple_of((index // tiles) * 16, 16)
        subs = pl.ds(start, 16)
        lanes = pl.ds(pl.multiple_of((index % tiles) * LANES, LANES), LANES)
        phases = [(cos_ref[k, subs, lanes], sin_ref[k, subs, lanes]) for k in range(4)]
        for box in range(boxes):
            real_sum = None
            for k, (phase_cos, phase_sin) in enumerate(phases):
                real, imag = [full_ref[8 * box + 2 * k + x, subs, lanes] for x in range(2)]
                terms = (phase_cos * real - phase_sin * imag, phase_cos * imag + phase_sin * real)
                if real_sum is None:
                    real_sum, imag_sum = terms
                else:
                    real_sum, imag_sum = real_sum + terms[0], imag_sum + terms[1]
            out_ref[0, 0, box, subs, lanes] = real_sum.astype(bf16)
            out_ref[1, 0, box, subs, lanes] = imag_sum.astype(bf16)
        return carry

    lax.fori_loop(0, (theta_rows // 16) * tiles, combine, 0)


def aggregate(held, first, halos, inner, outer, phi_matrix, phase_cos, phase_sin, flags=None):
    _, rows, _, polar, azimuths = held[0][0].shape
    theta_rows, fine = inner.shape[0], phi_matrix.shape[1]
    group = outer.shape[0]
    widths = [cols for _, cols in held]
    total = sum(widths)
    beside = halos.shape[2]
    masked = flags is not None
    return pl.pallas_call(
        functools.partial(aggregate_kernel, masked, group, first, widths),
        grid=(rows // 2, 1),
        in_specs=[pl.BlockSpec(memory_space=pltpu.SMEM)] * masked
        + [pl.BlockSpec((2, 2, cols, polar, azimuths), lambda i, j: (0, i, 0, 0, 0)) for cols in widths]
        + [
            pl.BlockSpec((2, 2, beside, azimuths), lambda i, j: (0, i, 0, 0)),
            pl.BlockSpec((theta_rows, polar), lambda i, j: (0, 0)),
            pl.BlockSpec((group, theta_rows, 4 * group), lambda i, j: (0, 0, 0)),
            pl.BlockSpec((azimuths, fine), lambda i, j: (0, 0)),
            pl.BlockSpec((4, theta_rows, fine), lambda i, j: (0, 0, 0)),
            pl.BlockSpec((4, theta_rows, fine), lambda i, j: (0, 0, 0)),
        ],
        out_specs=pl.BlockSpec((2, 1, total // 2, theta_rows, fine), lambda i, j: (0, i, 0, 0, 0)),
        out_shape=jax.ShapeDtypeStruct((2, rows // 2, total // 2, theta_rows, fine), jnp.bfloat16),
        scratch_shapes=[
            pltpu.VMEM((4 * total * theta_rows, azimuths), jnp.bfloat16),
            pltpu.VMEM((4 * total, theta_rows, fine), jnp.float32),
        ],
        compiler_params=pltpu.CompilerParams(vmem_limit_bytes=VMEM_BYTES),
        cost_estimate=cost(0.5 * rows * total / 4 + 1),
    )(*[flags] * masked, *[value for value, _ in held], halos, inner, outer, phi_matrix, phase_cos, phase_sin)


def runs_of(row, rows, own, sides):
    steps = [
        step
        for step in steps_of(row % 2)
        if (own if 0 <= row + step < rows else sides)
    ]
    runs = []
    for step in steps:
        kind = (abs(step) >= 2, step > 0 and abs(step) >= 2)
        if runs and runs[-1][0] == kind and runs[-1][2] == step:
            runs[-1][2] = step + 1
        else:
            runs.append([kind, step, step + 1])
    return [(kind[0], start, stop) for kind, start, stop in runs]


def translate_kernel(plan, odd_ref, dest_ref, *refs):
    own_pieces, swap_pieces, far_pieces, first, last, columns, rows, partial, final, whole = plan
    refs = list(refs)
    own_refs = [refs.pop(0) for _ in own_pieces]
    swap_refs = [refs.pop(0) for _ in swap_pieces]
    far_refs = [refs.pop(0) for _ in far_pieces]
    table_ref = refs.pop(0)
    partial_ref = refs.pop(0) if partial else None
    if whole:
        refs.pop(0)
    out_ref = refs.pop(0)
    source_ref, factor_ref = refs.pop(0), refs.pop(0)
    sum_ref = refs.pop(0) if final else None
    polar, azimuths = table_ref.shape[2], table_ref.shape[3]
    half = min(8, polar)
    even = odd_ref[0] == 0
    wide = last - first
    span = wide + 4
    f32 = jnp.float32
    at_once = 8 if wide % 8 == 0 else wide

    zero = jnp.zeros((polar, LANES), f32)

    def clear(row, carry):
        for col in range(span):
            if not 0 <= first - 2 + col < columns:
                for form in range(3):
                    source_ref[form, row, col] = zero
        return carry

    lax.fori_loop(0, rows + 4, clear, 0)

    def keep(row, col, real, imag, flag=None):
        real, imag = real.astype(f32), imag.astype(f32)
        if flag is not None:
            real, imag = real * flag, imag * flag
        source_ref[0, row, col] = real
        source_ref[1, row, col] = imag
        source_ref[2, row, col] = real + imag

    def tile(index, carry):
        lanes = pl.ds(pl.multiple_of(index * LANES, LANES), LANES)

        def keep_own(row, carry):
            for piece, (start, stop, raw) in enumerate(own_pieces):
                for col in range(max(start, first - 2), min(stop, last + 2)):
                    flag = dest_ref[row, col].astype(f32) if raw else None
                    keep(row + 2, col - (first - 2), *[own_refs[piece][x, row, col - start, :, lanes] for x in range(2)], flag)
            return carry

        def keep_sides(row, carry):
            def load(pieces, piece_refs, col):
                ref, at = [
                    (ref, col - start) for ref, (start, stop) in zip(piece_refs, pieces) if start <= col < stop
                ][0]
                return [ref[x, row, at, :, lanes] for x in range(2)]

            for col in range(max(0, first - 2), min(columns, last + 2)):
                swap, far = load(swap_pieces, swap_refs, col), load(far_pieces, far_refs, col)
                to = col - (first - 2)
                keep(row, to, *[jnp.where(even, far[x], swap[x]) for x in range(2)])
                keep(rows + 2 + row, to, *[jnp.where(even, swap[x], far[x]) for x in range(2)])
            return carry

        if own_pieces:
            lax.fori_loop(0, rows, keep_own, 0)
        if swap_pieces:
            lax.fori_loop(0, 2, keep_sides, 0)

        def keep_factors(block, carry):
            for code in [block * 4 + n for n in range(4)]:
                real = table_ref[0, code, :, lanes].astype(f32)
                imag = table_ref[1, code, :, lanes].astype(f32)
                factor_ref[0, code] = real
                factor_ref[1, code] = imag - real
                factor_ref[2, code] = imag + real
            return carry

        lax.fori_loop(0, len(far_offsets) // 4, keep_factors, 0)

        def part(index, carry):
            subs = pl.ds(pl.multiple_of((index % (polar // half)) * half, half), half)
            begin = (index // (polar // half)) * at_once
            for row in range(rows):

                def one_step(far_row, base, start, row=row):
                    cols = [q for q in range(-3, 4) if far_row or abs(q) >= 2]

                    def body(step, sums):
                        sums = [list(s) for s in sums]
                        found = {}
                        code = base + step * len(cols)
                        for n, step_col in enumerate(cols):
                            factor = [factor_ref[form, code + n, subs] for form in range(3)]
                            for dest in range(at_once):
                                if step_col not in steps_of(dest % 2):
                                    continue
                                col = dest + 2 + step_col
                                if col not in found:
                                    found[col] = [
                                        source_ref[form, row + 2 + start + step, begin + col, subs]
                                        for form in range(3)
                                    ]
                                real, imag, both = found[col]
                                terms = (both * factor[0], real * factor[1], imag * factor[2])
                                sums[dest] = [s + t for s, t in zip(sums[dest], terms)]
                        return tuple(tuple(s) for s in sums)

                    return body

                nothing = jnp.zeros((half, LANES), f32)
                sums = tuple((nothing,) * 3 for _ in range(at_once))
                for far_row, start, stop in runs_of(row, rows, bool(own_pieces), bool(swap_pieces)):
                    base = code_of[start, -3]
                    sums = lax.fori_loop(0, stop - start, one_step(far_row, base, start), sums)
                for dest in range(at_once):
                    shared, cross, other = sums[dest]
                    pair = [shared - other, shared + cross]
                    for x in range(2):
                        value = pair[x]
                        if partial:
                            value = value + partial_ref[x, row, begin + dest, subs, lanes]
                        if final:
                            flag = dest_ref[row, first + begin + dest].astype(f32)
                            sum_ref[x, row, begin + dest, subs] = value * flag
                        else:
                            out_ref[x, row, begin + dest, subs, lanes] = value
            return carry

        lax.fori_loop(0, (polar // half) * (wide // at_once), part, 0)

        def finish(row, carry):
            for x in range(2):
                for dest in range(wide):
                    out_ref[x, row, dest, :, lanes] = sum_ref[x, row, dest].astype(jnp.bfloat16)
            return carry

        if final:
            lax.fori_loop(0, rows, finish, 0)
        return carry

    lax.fori_loop(0, azimuths // LANES, tile, 0)


def translate(own, sides, table, dest, odd, first, last, partial=None, final=True, whole=None, raw=False, part=(0, 1)):
    rows, columns = dest.shape
    polar, azimuths = table.shape[2], table.shape[3]
    block = min(16, polar)
    edge = rows // 2 - 1
    wide = last - first
    steps = polar // block // part[1]
    skip = part[0] * steps

    own_pieces = [(0, columns, raw)] if own else []
    swap_side, far_side = [
        [chunk for chunk in side if chunk[1] < last + 2 and chunk[2] > first - 2] for side in sides or ([], [])
    ]
    at = first // wide
    operands = list(own)
    specs = [
        pl.BlockSpec((2, rows, stop - start, block, azimuths), lambda t, odd, dest: (0, 0, 0, t + skip, 0))
        for start, stop, _ in own_pieces
    ]
    for side, place in ((swap_side, lambda odd: odd), (far_side, lambda odd: 1 - odd)):
        operands += [held for held, start, stop in side]
        specs += [
            pl.BlockSpec(
                (2, 2, stop - start, block, azimuths),
                lambda t, odd, dest, place=place: (0, place(odd[0]) * edge, 0, t + skip, 0),
            )
            for held, start, stop in side
        ]
    operands.append(table)
    specs.append(pl.BlockSpec((2, len(far_offsets), block, azimuths), lambda t, odd, dest: (0, 0, t + skip, 0)))
    out_spec = pl.BlockSpec((2, rows, wide, block, azimuths), lambda t, odd, dest: (0, 0, at, t + skip, 0))
    if partial is not None:
        operands.append(partial)
        specs.append(out_spec)
    aliases = {}
    if whole is not None:
        operands.append(whole)
        specs.append(pl.BlockSpec(memory_space=pl.ANY))
        aliases = {len(operands) + 1: 0}
    kind = jnp.bfloat16 if final else jnp.float32
    scratch = [
        pltpu.VMEM((3, rows + 4, wide + 4, block, LANES), jnp.float32),
        pltpu.VMEM((3, len(far_offsets), block, LANES), jnp.float32),
    ]
    if final:
        scratch.append(pltpu.VMEM((2, rows, wide, block, LANES), jnp.float32))
    swap_pieces, far_pieces = [[chunk[1:] for chunk in side] for side in (swap_side, far_side)]
    plan = (own_pieces, swap_pieces, far_pieces, first, last, columns, rows, partial is not None, final, whole is not None)
    share = ((2 / 3 if rows > 2 else 2 / 9) if own else 0) + ((1 / 3 if rows > 2 else 7 / 9) if sides else 0)
    return pl.pallas_call(
        functools.partial(translate_kernel, plan),
        grid_spec=pltpu.PrefetchScalarGridSpec(
            num_scalar_prefetch=2,
            grid=(steps,),
            in_specs=specs,
            out_specs=out_spec,
            scratch_shapes=scratch,
        ),
        out_shape=jax.ShapeDtypeStruct((2, rows, columns, polar, azimuths), kind),
        input_output_aliases=aliases,
        compiler_params=pltpu.CompilerParams(vmem_limit_bytes=VMEM_BYTES),
        cost_estimate=cost(22 * share * wide / columns / part[1] + 1),
    )(odd, dest, *operands)


def local(pattern, occupied, trans_fine, trans_coarse, theta_weights, phi_matrix, child_phase):
    _, count_rows, count_cols, polar, azimuths = pattern.shape
    groups = lax.axis_size("box")
    odd = (lax.axis_index("box") % 2).astype(jnp.int32).reshape(1)
    partner = [(i, i ^ 1) for i in range(groups)]
    onward = [(i, i + 2) for i in range(0, groups - 2, 2)] + [(i, i - 2) for i in range(3, groups, 2)]
    group = count_cols // 4
    widths = [3 * group // 2, group, 3 * group // 2]
    starts = [0, widths[0], widths[0] + group, count_cols]

    def flat(held):
        return held.reshape(2, count_rows, -1, azimuths)

    def placed(held, cols):
        ends = [sum(cols[: k + 1]) for k in range(len(cols))]
        return [(value, end - size, end) for value, size, end in zip(held, cols, ends)]

    def send(value, pairs):
        return lax.ppermute(value, "box", pairs)

    fine_plan = (trans_fine, occupied, odd)
    occupied_coarse = jnp.max(occupied.reshape(count_rows // 2, 2, count_cols // 2, 2), axis=(1, 3))
    coarse_plan = (trans_coarse, occupied_coarse, odd)
    half = count_cols // 2

    own0 = mask_first(pattern, occupied, widths[0])
    rest, flags, own0 = lax.optimization_barrier((pattern, occupied, own0))
    flags = flags.astype(jnp.bfloat16)[None, :, :, None, None]

    def chunk(values, k):
        return values[:, :, starts[k] : starts[k + 1]] * flags[:, :, starts[k] : starts[k + 1]]

    swap0 = send(own0, partner)
    edges = jnp.concatenate([rest[:, :, :, :2], rest[:, :, :, -2:]], axis=3) * flags
    beside = halo(edges)
    fine_sums = translate([rest], None, *fine_plan, 0, count_cols, final=False, raw=True)
    own1, own2 = chunk(rest, 1), chunk(rest, 2)
    swap0, fine_sums, beside, own1, own2, rest, child_phase = lax.optimization_barrier(
        (swap0, fine_sums, beside, own1, own2, rest, child_phase)
    )

    own_halo = jnp.concatenate(beside, axis=3).reshape(2, count_rows, -1, polar, azimuths)
    swap1 = send(jnp.concatenate([own1, own_halo], axis=2), partner)
    far0 = send(swap0, onward)
    phases = (jnp.cos(child_phase), jnp.sin(child_phase))
    fixed = (*bands(theta_weights, polar, group), phi_matrix, *phases)
    coarse_own = aggregate([(rest, count_cols)], 0, flat(own_halo), *fixed, flags=occupied)
    swap0, swap1, far0, coarse_own, own2 = lax.optimization_barrier((swap0, swap1, far0, coarse_own, own2))

    swap2 = send(own2, partner)
    far1 = send(swap1, onward)
    swap_halo = flat(swap1[:, :, widths[1] :])
    coarse_swap = [aggregate([(swap0, widths[0]), (swap1, widths[1])], 0, swap_halo, *fixed)]
    coarse_sums = translate([coarse_own], None, *coarse_plan, 0, half, final=False)
    swap2, far1, coarse_swap, swap_halo, coarse_sums = lax.optimization_barrier(
        (swap2, far1, coarse_swap, swap_halo, coarse_sums)
    )

    far2 = send(swap2, onward)
    far_halo = flat(far1[:, :, widths[1] :])
    coarse_far = [aggregate([(far0, widths[0]), (far1, widths[1])], 0, far_halo, *fixed)]
    coarse_swap.append(aggregate([(swap2, widths[2])], starts[2], swap_halo, *fixed))
    early = [placed(held, widths[:2]) for held in ((swap0, swap1), (far0, far1))]
    local_fine = translate([], early, *fine_plan, 0, half, partial=fine_sums)
    far2, coarse_far, coarse_swap, local_fine, fine_sums = lax.optimization_barrier(
        (far2, coarse_far, coarse_swap, local_fine, fine_sums)
    )

    coarse_far.append(aggregate([(far2, widths[2])], starts[2], far_halo, *fixed))
    coarse_sides = [placed(held, [starts[2] // 2, widths[2] // 2]) for held in (coarse_swap, coarse_far)]
    local_coarse = translate([], coarse_sides, *coarse_plan, 0, half, partial=coarse_sums)
    fine_sides = [placed(held, widths) for held in ((swap0, swap1, swap2), (far0, far1, far2))]
    local_fine = translate([], fine_sides, *fine_plan, half, count_cols, partial=fine_sums, whole=local_fine)
    return local_fine, local_coarse


def solution(mesh):
    return jax.shard_map(
        local,
        mesh=mesh,
        in_specs=(
            P(None, "box", None, "dir", None),
            P("box", None),
            P(None, None, "dir", None),
            P(None, None, "dir", None),
            P("dir", None),
            P(),
            P(None, "dir", None),
        ),
        out_specs=(P(None, "box", None, "dir", None), P(None, "box", None, "dir", None)),
        check_vma=False,
    )
```
